32 devices in a mesh: grp: 1, gx: 16 (over z, y, x), gy: 2 (over core).
Axes of the slice: x: 2, y: 2, z: 4, core: 2. Of those that a mesh axis runs over, the one named last changes fastest.
Arguments:
- voltages: bfloat16 [2, 64, 8, 256, 256], P(None, 'grp', None, 'gx', 'gy'), may hold values from -6 to 6
Outputs:
- visibility: float32 [2, 64, 512, 512], P(None, ('grp', 'gy'), 'gx')
The draws below stay inside these ranges and needn't reach their ends.
All inputs are finite; a program needn't handle non-finite values.
Results may differ from the reference program's by a relative error of at most 0.0024.
Values may be sent and summed in bfloat16 or wider, within the bound.
A program may use at most 128 MiB of HBM per device.

```python
import math
import jax
import jax.numpy as jnp
from jax import lax

NA = 256
C = 64
T_SIZE = 8
NB = 512


def level_of(own_key, shape, pieces, least, high):
    gain = 1.0
    for axis_at, parts in pieces:
        heights = jax.random.uniform(jax.random.fold_in(jax.random.fold_in(own_key, 6), axis_at), (parts,), jnp.float32, least / len(pieces), high / len(pieces))
        gain = gain * jnp.repeat(jnp.exp(heights), shape[axis_at] // parts).reshape((-1,) + (1,) * (len(shape) - 1 - axis_at))
    return gain


def normal_values(stream_key, shape, spread, bound, cuts=(), held_as=jnp.bfloat16):
    gain = level_of(stream_key, shape, cuts, -0.22, 0.18) if cuts else 1.0
    values = jax.random.normal(stream_key, shape, jnp.float32) * spread * gain
    return jnp.minimum(jnp.maximum(values, -bound), bound).astype(held_as)


def setup_inputs(seed: int = 0, part: int = 0) -> dict:
    streams_of = jax.random.split(jax.random.key(seed), 2)
    part_splits = jax.random.split(jax.random.fold_in(streams_of[1], part), 2)
    return {
        "voltages": normal_values(part_splits[0], (2, C, T_SIZE, NA, NA), 1.0, 6.0, ((3, 16), (4, 2))),
    }


def dft_table(row_count, col_count, sign_factor, scale_factor, out_type):
    row_index = lax.iota(jnp.int32, row_count)[:, None]
    col_index = lax.iota(jnp.int32, col_count)[None, :]
    phase_index = (row_index * col_index) % NB
    angles = (2.0 * math.pi / NB) * phase_index.astype(jnp.float32)
    return (jnp.cos(angles) * scale_factor).astype(out_type), (sign_factor * jnp.sin(angles) * scale_factor).astype(out_type)


def reference(voltages):
    fwd_re, fwd_im = dft_table(NA, NB, -1.0, 1.0, jnp.bfloat16)
    fwd_re = fwd_re.astype(jnp.float32)
    fwd_im = fwd_im.astype(jnp.float32)
    inv_re, inv_im = dft_table(NB, NB, 1.0, 1.0 / NB, jnp.float32)
    out_re, out_im = dft_table(NB, NB, 1.0, 1.0 / (NB * T_SIZE * NA), jnp.float32)
    high = lax.Precision.HIGHEST

    def one_channel(channel_volts):
        volt_re = channel_volts[0].astype(jnp.float32)
        volt_im = channel_volts[1].astype(jnp.float32)
        beam_re = jnp.einsum('txy,yv->txv', volt_re, fwd_re, precision=high) - jnp.einsum('txy,yv->txv', volt_im, fwd_im, precision=high)
        beam_im = jnp.einsum('txy,yv->txv', volt_re, fwd_im, precision=high) + jnp.einsum('txy,yv->txv', volt_im, fwd_re, precision=high)
        beam_re = lax.optimization_barrier(beam_re.astype(jnp.bfloat16)).astype(jnp.float32)
        beam_im = lax.optimization_barrier(beam_im.astype(jnp.bfloat16)).astype(jnp.float32)
        full_re = jnp.einsum('txv,xu->tuv', beam_re, fwd_re, precision=high) - jnp.einsum('txv,xu->tuv', beam_im, fwd_im, precision=high)
        full_im = jnp.einsum('txv,xu->tuv', beam_re, fwd_im, precision=high) + jnp.einsum('txv,xu->tuv', beam_im, fwd_re, precision=high)
        power = jnp.sum(full_re * full_re + full_im * full_im, axis=0)
        lag_re = jnp.einsum('uv,ul->lv', power, inv_re, precision=high)
        lag_im = jnp.einsum('uv,ul->lv', power, inv_im, precision=high)
        vis_re = jnp.dot(lag_re, out_re, precision=high) - jnp.dot(lag_im, out_im, precision=high)
        vis_im = jnp.dot(lag_re, out_im, precision=high) + jnp.dot(lag_im, out_re, precision=high)
        return jnp.stack([vis_re, vis_im])

    result = lax.map(one_channel, jnp.moveaxis(voltages, 1, 0))
    return jnp.moveaxis(result, 0, 1)
```

```python
import functools
import math

import jax
import jax.numpy as jnp
import ml_dtypes
import numpy as np
from jax import lax
from jax.experimental import pallas as pl
from jax.experimental.pallas import tpu as pltpu
from jax.sharding import PartitionSpec as P

NA = 256
T_SIZE = 8
NB = 512


def dft_table(row_count, col_count, sign_factor, scale_factor, out_type):
    row_index = lax.iota(jnp.int32, row_count)[:, None]
    col_index = lax.iota(jnp.int32, col_count)[None, :]
    phase_index = row_index * col_index % NB
    angles = 2.0 * math.pi / NB * phase_index.astype(jnp.float32)
    return (
        (jnp.cos(angles) * scale_factor).astype(out_type),
        (sign_factor * jnp.sin(angles) * scale_factor).astype(out_type),
    )


def plain(voltages):
    high = lax.Precision.HIGHEST
    f32 = jnp.float32
    fwd_re, fwd_im = dft_table(NA, NB, -1.0, 1.0, jnp.bfloat16)
    inv_re, inv_im = dft_table(NB, NB, 1.0, 1.0 / NB, jnp.float32)
    out_re, out_im = dft_table(NB, NB, 1.0, 1.0 / (NB * T_SIZE * NA), jnp.float32)
    turned = lax.all_to_all(voltages, "gy", split_axis=1, concat_axis=4, tiled=True)
    stacks, channels, snapshots, x_rows, y_cols = turned.shape
    gx_size = lax.axis_size("gx")
    item_count = channels * snapshots // gx_size
    group_snaps = min(item_count, snapshots)
    group_count = item_count // group_snaps
    item_rows = turned.reshape(2, channels * snapshots, x_rows, y_cols)
    received = lax.all_to_all(item_rows, "gx", split_axis=1, concat_axis=2, tiled=True)
    received = received.reshape(2, group_count, group_snaps, NA, NA)
    beam_re = jnp.einsum(
        "gtxy,yv->gtxv", received[0], fwd_re, preferred_element_type=f32
    ) - jnp.einsum("gtxy,yv->gtxv", received[1], fwd_im, preferred_element_type=f32)
    beam_im = jnp.einsum(
        "gtxy,yv->gtxv", received[0], fwd_im, preferred_element_type=f32
    ) + jnp.einsum("gtxy,yv->gtxv", received[1], fwd_re, preferred_element_type=f32)
    beam_re = beam_re.astype(jnp.bfloat16)
    beam_im = beam_im.astype(jnp.bfloat16)
    full_re = jnp.einsum("gtxv,xu->gtuv", beam_re, fwd_re, preferred_element_type=f32) - jnp.einsum(
        "gtxv,xu->gtuv", beam_im, fwd_im, preferred_element_type=f32
    )
    full_im = jnp.einsum("gtxv,xu->gtuv", beam_re, fwd_im, preferred_element_type=f32) + jnp.einsum(
        "gtxv,xu->gtuv", beam_im, fwd_re, preferred_element_type=f32
    )
    power = jnp.sum(full_re * full_re + full_im * full_im, axis=1)
    per_channel = gx_size * group_count // channels
    lag_re = jnp.einsum("guv,ul->glv", power, inv_re, precision=high)
    lag_im = jnp.einsum("guv,ul->glv", power, inv_im, precision=high)
    partial_value = jnp.stack([lag_re, lag_im], axis=1)[None]
    gathered_lags = lax.all_to_all(partial_value, "gx", split_axis=3, concat_axis=0, tiled=True)
    lag_rows_dev = gathered_lags.shape[3]
    lag_sums = jnp.sum(gathered_lags.reshape(channels, per_channel, 2, lag_rows_dev, NB), axis=1)
    vis_re = jnp.einsum("clv,vm->clm", lag_sums[:, 0], out_re, precision=high) - jnp.einsum(
        "clv,vm->clm", lag_sums[:, 1], out_im, precision=high
    )
    vis_im = jnp.einsum("clv,vm->clm", lag_sums[:, 0], out_im, precision=high) + jnp.einsum(
        "clv,vm->clm", lag_sums[:, 1], out_re, precision=high
    )
    return jnp.stack([vis_re, vis_im])


HALF = NB // 2
MESH = pl.DeviceIdType.MESH
T_PART = 4
GROUP = 4


def pair_of(x):
    high = x.astype(ml_dtypes.bfloat16)
    return np.stack([high, (x - high.astype(np.float64)).astype(ml_dtypes.bfloat16)])


def fixed_tables():
    turn = 2.0 * np.pi / NB
    a, b = np.arange(NA), np.arange(HALF)
    cos = np.cos(turn * (np.outer(a, b) % NB))
    sin = np.sin(turn * (np.outer(a, b) % NB))
    alt = 1.0 - 2.0 * (np.arange(NB) % 2)
    sin[:, 0] = alt[:NA]
    first = np.concatenate([cos, sin], axis=1).astype(ml_dtypes.bfloat16)
    second = np.ascontiguousarray(first.T)
    lag = np.outer(np.arange(NB), b) % NB
    lag_cos = 2.0 * np.cos(turn * lag) / NB
    lag_cos[:, 0] = 1.0 / NB
    lag_sin = 4.0 * np.sin(turn * lag) / NB
    out_phase = lag.T
    out_sin = np.sin(turn * out_phase)
    out_sin[0] = alt
    out = np.concatenate([np.cos(turn * out_phase), out_sin]) / (NB * T_SIZE * NA)
    return first, second, pair_of(lag_cos), pair_of(lag_sin), pair_of(out)


def flip(value, mask, bits):
    out = 0
    for k in range(bits):
        unit = 2**k
        out = out + lax.rem(lax.div(value, unit) + lax.div(mask, unit), 2) * unit
    return out


def rest(x):
    return x - x.astype(jnp.bfloat16).astype(jnp.float32)


def kernel(gx_size, gy_size, v_ref, t1_ref, t2_ref, tc_ref, ts_ref, to_ref, out_ref, rv, t1, t2, tc, ts, to, even, odd, nyq,
           hbuf, hrecv, all_in, tab_sem, v_send, v_recv, h_send, h_recv):
    f32, bf16 = jnp.float32, jnp.bfloat16
    _, channels, snaps, x_rows, y_cols = v_ref.shape
    count = gx_size * gy_size
    bits = count.bit_length() - 1
    owned = channels // count
    lag_rows = NB // gx_size
    grp, gx, gy = lax.axis_index("grp"), lax.axis_index("gx"), lax.axis_index("gy")
    me = gx * gy_size + gy
    parts = snaps // T_PART

    barrier = pltpu.get_barrier_semaphore()
    mirror_mask = gx_size * 3 // 4
    mirror = flip(gx, mirror_mask, gx_size.bit_length() - 1)
    pl.semaphore_signal(barrier, inc=1, device_id=(grp, mirror, 0), device_id_type=MESH)
    for k in range(1, gx_size):
        pl.semaphore_signal(barrier, inc=1, device_id=(grp, lax.rem(gx + k, gx_size), 1), device_id_type=MESH)

    @pl.when(gy == 0)
    def _():
        pl.semaphore_signal(barrier, inc=1, device_id=(grp, gx, 1), device_id_type=MESH)

    x_at = pl.ds(pl.multiple_of(gx * x_rows, x_rows), x_rows)
    y_at = pl.ds(pl.multiple_of(gy * y_cols, y_cols), y_cols)

    def channel_of(ox, oy, ch):
        return oy * (channels // gy_size) + ox * owned + ch

    def send_block(ox, oy, ch, part):
        times = pl.ds(part * T_PART, T_PART)
        pltpu.make_async_remote_copy(
            src_ref=v_ref.at[:, channel_of(ox, oy, ch), times],
            dst_ref=rv.at[ch, :, times, x_at, y_at],
            send_sem=v_send,
            recv_sem=v_recv.at[ch * parts + part],
            device_id=(grp, ox, oy),
            device_id_type=MESH,
        ).start()

    @pl.when(gy == 0)
    def _():
        pl.semaphore_wait(barrier, gy_size)
        for ch in range(owned):
            for part in range(parts):
                for oy in range(gy_size):
                    send_block(mirror, oy, ch, part)

    tables = [
        pltpu.make_async_copy(src, dst, tab_sem.at[n])
        for n, (src, dst) in enumerate(((t1_ref, t1), (t2_ref, t2), (tc_ref, tc), (ts_ref, ts), (to_ref, to)))
    ]
    for copy in tables:
        copy.start()

    @pl.when(gy == 1)
    def _():
        pl.semaphore_wait(barrier, count - 1)
        pl.semaphore_signal(all_in, inc=1, device_id=(grp, gx, 0), device_id_type=MESH)

    @pl.when(gy == 0)
    def _():
        pl.semaphore_wait(all_in, 1)

    for ch in range(owned):
        for part in range(parts):
            times = pl.ds(part * T_PART, T_PART)

            def send(n, carry):
                s = lax.rem(n, 2) * (count // 2) + lax.div(n, 2)
                other = flip(me, s, bits)

                @pl.when((gy == 1) | (lax.div(s, gy_size) != mirror_mask))
                def _():
                    send_block(lax.div(other, gy_size), lax.rem(other, gy_size), ch, part)

                return carry

            lax.fori_loop(1, count, send, 0)
            pltpu.make_async_copy(
                v_ref.at[:, channel_of(gx, gy, ch), times], rv.at[ch, :, times, x_at, y_at], v_recv.at[ch * parts + part]
            ).start()

    for copy in tables:
        copy.wait()

    lane0 = lax.broadcasted_iota(jnp.int32, (NA, HALF), 1) == 0
    row0 = lax.broadcasted_iota(jnp.int32, (HALF, HALF), 0) == 0
    dot = functools.partial(jnp.dot, preferred_element_type=f32)

    for ch in range(owned):
        even[...] = jnp.zeros_like(even)
        odd[...] = jnp.zeros_like(odd)
        nyq[...] = jnp.zeros_like(nyq)
        for part in range(parts):
            landed = rv.at[ch, :, pl.ds(part * T_PART, T_PART)]
            pltpu.make_async_copy(landed, landed, v_recv.at[ch * parts + part]).wait()

            def snapshot(t, carry):
                re = dot(rv[ch, 0, t], t1[...])
                im = dot(rv[ch, 1, t], t1[...])
                cr, sr, ci, si = re[:, :HALF], re[:, HALF:], im[:, :HALF], im[:, HALF:]
                halves = (
                    (cr + jnp.where(lane0, 0.0, si), ci - jnp.where(lane0, 0.0, sr)),
                    (jnp.where(lane0, sr, cr - si), jnp.where(lane0, si, ci + sr)),
                )
                for n, (b_re, b_im) in enumerate(halves):
                    at = slice(n * HALF, (n + 1) * HALF)
                    re = dot(t2[...], b_re.astype(bf16))
                    im = dot(t2[...], b_im.astype(bf16))
                    cr, sr, ci, si = re[:HALF], re[HALF:], im[:HALF], im[HALF:]
                    nyq[:, at] += sr[:8] * sr[:8] + si[:8] * si[:8]
                    sr, si = jnp.where(row0, 0.0, sr), jnp.where(row0, 0.0, si)
                    even[:, at] += (cr * cr + ci * ci) + (sr * sr + si * si)
                    odd[:, at] += cr * si - ci * sr
                return carry

            lax.fori_loop(part * T_PART, (part + 1) * T_PART, snapshot, 0)

        e_hi = even[...].astype(bf16)
        e_lo = (even[...] - e_hi.astype(f32)).astype(bf16)
        o_hi = odd[...].astype(bf16)
        o_lo = (odd[...] - o_hi.astype(f32)).astype(bf16)
        alt = 1.0 - 2.0 * lax.rem(lax.broadcasted_iota(jnp.int32, (HALF, 1), 0), 2).astype(f32)
        top = nyq[0:1, :] * (1.0 / NB)
        mask = lax.broadcasted_iota(jnp.int32, (HALF, HALF), 1) == 0
        for n in range(2):
            rows = slice(n * HALF, (n + 1) * HALF)
            h_re = dot(tc[0, rows], e_hi) + dot(tc[0, rows], e_lo) + dot(tc[1, rows], e_hi) + alt * top
            h_im = dot(ts[0, rows], o_hi) + dot(ts[0, rows], o_lo) + dot(ts[1, rows], o_hi)
            rp, rm, ip, im = h_re[:, :HALF], h_re[:, HALF:], h_im[:, :HALF], h_im[:, HALF:]
            slots = [
                jnp.where(mask, rp, rp + rm),
                jnp.where(mask, rm, im - ip),
                jnp.where(mask, ip, ip + im),
                jnp.where(mask, im, rp - rm),
            ]
            if n == 0:
                slots[1] = jnp.where(row0 & ~mask, rest(rp - rm), slots[1])
                slots[2] = jnp.where(row0, rest(slots[0]), slots[2])
                slots[3] = jnp.where(row0 & mask, rest(rm), slots[3])
            for k, slot in enumerate(slots):
                hbuf[ch, rows, k * HALF : (k + 1) * HALF] = slot.astype(bf16)

        def send_lags(n, carry):
            s = lax.rem(n, 2) * (gx_size // 2) + lax.div(n, 2)
            other = flip(gx, s, gx_size.bit_length() - 1)
            pltpu.make_async_remote_copy(
                src_ref=hbuf.at[ch, pl.ds(pl.multiple_of(other * lag_rows, lag_rows), lag_rows)],
                dst_ref=hrecv.at[ch, gx],
                send_sem=h_send.at[ch],
                recv_sem=h_recv.at[ch, lax.div(gx, GROUP)],
                device_id=(grp, other, gy),
                device_id_type=MESH,
            ).start()
            return carry

        lax.fori_loop(1, gx_size, send_lags, 0)
        pltpu.make_async_copy(
            hbuf.at[ch, pl.ds(pl.multiple_of(gx * lag_rows, lag_rows), lag_rows)], hrecv.at[ch, gx], h_recv.at[ch, lax.div(gx, GROUP)]
        ).start()

    own_group = lax.div(gx, GROUP)
    zero = jnp.zeros((gx_size, HALF), bf16)
    left = lax.broadcasted_iota(jnp.int32, (gx_size, HALF), 1) == 0

    for ch in range(owned):

        def finish(n, carry):
            group = flip(own_group, n, (gx_size // GROUP).bit_length() - 1)
            sources = pl.ds(group * GROUP, GROUP)
            landed = hrecv.at[ch, sources]
            pltpu.make_async_copy(landed, landed, h_recv.at[ch, group]).wait()
            for part in range(2):
                x = hrecv[ch, sources, :, part * NB : (part + 1) * NB].reshape(GROUP * lag_rows, NB)
                y = dot(x, to[0]) + dot(x, to[1])
                out_ref[part, sources, ch] = y.reshape(GROUP, lag_rows, NB)
            return carry

        lax.fori_loop(0, gx_size // GROUP, finish, 0)

        @pl.when(gx == 0)
        def _():
            row = hrecv[ch, :, 0, :]
            a_hi, s1, a_lo, s3 = (row[:, k * HALF : (k + 1) * HALF] for k in range(4))
            for part in range(2):
                total = 0.0
                for a, b in ((a_hi, s1), (a_lo, s3)):
                    x = [a, jnp.where(left, b, zero)] if part == 0 else [zero, jnp.where(left, zero, b)]
                    x = jnp.concatenate(x, axis=1)
                    total += dot(x, to[0]) + dot(x, to[1])
                out_ref[part, :, ch, 0, :] = total

    for ch in range(owned):
        sent = hbuf.at[ch, pl.ds(0, (gx_size - 1) * lag_rows)]
        pltpu.make_async_copy(sent, sent, h_send.at[ch]).wait()
    sent = v_ref.at[:, pl.ds(0, channels - owned)]
    pltpu.make_async_copy(sent, sent, v_send).wait()


def fused(gx_size, gy_size, voltages):
    _, channels, snaps, _, _ = voltages.shape
    owned = channels // (gx_size * gy_size)
    lag_rows = NB // gx_size
    tables = [jnp.asarray(table) for table in fixed_tables()]
    bf16, f32 = jnp.bfloat16, jnp.float32
    dma = pltpu.SemaphoreType.DMA
    out = pl.pallas_call(
        functools.partial(kernel, gx_size, gy_size),
        out_shape=pltpu.VMEM((2, gx_size, owned, lag_rows, NB), f32),
        in_specs=[pl.BlockSpec(memory_space=pltpu.HBM)] * 6,
        out_specs=pl.BlockSpec(memory_space=pltpu.VMEM),
        scratch_shapes=[
            pltpu.VMEM((owned, 2, snaps, NA, NA), bf16),
            *[pltpu.VMEM(table.shape, bf16) for table in tables],
            pltpu.VMEM((HALF, NB), f32),
            pltpu.VMEM((HALF, NB), f32),
            pltpu.VMEM((8, NB), f32),
            pltpu.VMEM((owned, NB, 2 * NB), bf16),
            pltpu.VMEM((owned, gx_size, lag_rows, 2 * NB), bf16),
            pltpu.SemaphoreType.REGULAR,
            dma((5,)),
            dma,
            dma((owned * snaps // T_PART,)),
            dma((owned,)),
            dma((owned, gx_size // GROUP)),
        ],
        compiler_params=pltpu.CompilerParams(
            collective_id=0, has_side_effects=True, vmem_limit_bytes=40 * 2**20
        ),
        cost_estimate=pl.CostEstimate(flops=2 * 10**10, bytes_accessed=12 * 2**20, transcendentals=0),
    )(*[pltpu.with_memory_space_constraint(x, pltpu.HBM) for x in (voltages, *tables)])
    return out.reshape(2, gx_size * owned, lag_rows, NB)


def local(gx_size, gy_size, voltages):
    _, channels, snaps, x_rows, y_cols = voltages.shape
    count = gx_size * gy_size
    even_split = count & (count - 1) == 0 and gx_size >= 4 and gy_size == 2 and channels % count == 0
    whole_tiles = x_rows % 16 == 0 and y_cols % 128 == 0 and (NB // gx_size) % 16 == 0 and snaps % T_PART == 0
    if even_split and whole_tiles:
        return fused(gx_size, gy_size, voltages)
    return plain(voltages)


def solution(mesh):
    return jax.shard_map(
        functools.partial(local, mesh.shape["gx"], mesh.shape["gy"]),
        mesh=mesh,
        in_specs=(P(None, "grp", None, "gx", "gy"),),
        out_specs=P(None, ("grp", "gy"), "gx", None),
        check_vma=False,
    )
```

```python
import functools
import math

import jax
import jax.numpy as jnp
import ml_dtypes
import numpy as np
from jax import lax
from jax.experimental import pallas as pl
from jax.experimental.pallas import tpu as pltpu
from jax.sharding import PartitionSpec as P

NA = 256
T_SIZE = 8
NB = 512


def dft_table(row_count, col_count, sign_factor, scale_factor, out_type):
    row_index = lax.iota(jnp.int32, row_count)[:, None]
    col_index = lax.iota(jnp.int32, col_count)[None, :]
    phase_index = row_index * col_index % NB
    angles = 2.0 * math.pi / NB * phase_index.astype(jnp.float32)
    return (
        (jnp.cos(angles) * scale_factor).astype(out_type),
        (sign_factor * jnp.sin(angles) * scale_factor).astype(out_type),
    )


def plain(voltages):
    high = lax.Precision.HIGHEST
    f32 = jnp.float32
    fwd_re, fwd_im = dft_table(NA, NB, -1.0, 1.0, jnp.bfloat16)
    inv_re, inv_im = dft_table(NB, NB, 1.0, 1.0 / NB, jnp.float32)
    out_re, out_im = dft_table(NB, NB, 1.0, 1.0 / (NB * T_SIZE * NA), jnp.float32)
    turned = lax.all_to_all(voltages, "gy", split_axis=1, concat_axis=4, tiled=True)
    stacks, channels, snapshots, x_rows, y_cols = turned.shape
    gx_size = lax.axis_size("gx")
    item_count = channels * snapshots // gx_size
    group_snaps = min(item_count, snapshots)
    group_count = item_count // group_snaps
    item_rows = turned.reshape(2, channels * snapshots, x_rows, y_cols)
    received = lax.all_to_all(item_rows, "gx", split_axis=1, concat_axis=2, tiled=True)
    received = received.reshape(2, group_count, group_snaps, NA, NA)
    beam_re = jnp.einsum(
        "gtxy,yv->gtxv", received[0], fwd_re, preferred_element_type=f32
    ) - jnp.einsum("gtxy,yv->gtxv", received[1], fwd_im, preferred_element_type=f32)
    beam_im = jnp.einsum(
        "gtxy,yv->gtxv", received[0], fwd_im, preferred_element_type=f32
    ) + jnp.einsum("gtxy,yv->gtxv", received[1], fwd_re, preferred_element_type=f32)
    beam_re = beam_re.astype(jnp.bfloat16)
    beam_im = beam_im.astype(jnp.bfloat16)
    full_re = jnp.einsum("gtxv,xu->gtuv", beam_re, fwd_re, preferred_element_type=f32) - jnp.einsum(
        "gtxv,xu->gtuv", beam_im, fwd_im, preferred_element_type=f32
    )
    full_im = jnp.einsum("gtxv,xu->gtuv", beam_re, fwd_im, preferred_element_type=f32) + jnp.einsum(
        "gtxv,xu->gtuv", beam_im, fwd_re, preferred_element_type=f32
    )
    power = jnp.sum(full_re * full_re + full_im * full_im, axis=1)
    per_channel = gx_size * group_count // channels
    lag_re = jnp.einsum("guv,ul->glv", power, inv_re, precision=high)
    lag_im = jnp.einsum("guv,ul->glv", power, inv_im, precision=high)
    partial_value = jnp.stack([lag_re, lag_im], axis=1)[None]
    gathered_lags = lax.all_to_all(partial_value, "gx", split_axis=3, concat_axis=0, tiled=True)
    lag_rows_dev = gathered_lags.shape[3]
    lag_sums = jnp.sum(gathered_lags.reshape(channels, per_channel, 2, lag_rows_dev, NB), axis=1)
    vis_re = jnp.einsum("clv,vm->clm", lag_sums[:, 0], out_re, precision=high) - jnp.einsum(
        "clv,vm->clm", lag_sums[:, 1], out_im, precision=high
    )
    vis_im = jnp.einsum("clv,vm->clm", lag_sums[:, 0], out_im, precision=high) + jnp.einsum(
        "clv,vm->clm", lag_sums[:, 1], out_re, precision=high
    )
    return jnp.stack([vis_re, vis_im])


HALF = NB // 2
MESH = pl.DeviceIdType.MESH
T_PART = 4
GROUP = 4


def pair_of(x):
    high = x.astype(ml_dtypes.bfloat16)
    return np.stack([high, (x - high.astype(np.float64)).astype(ml_dtypes.bfloat16)])


def fixed_tables():
    turn = 2.0 * np.pi / NB
    a, b = np.arange(NA), np.arange(HALF)
    cos = np.cos(turn * (np.outer(a, b) % NB))
    sin = np.sin(turn * (np.outer(a, b) % NB))
    alt = 1.0 - 2.0 * (np.arange(NB) % 2)
    sin[:, 0] = alt[:NA]
    first = np.concatenate([cos, sin], axis=1).astype(ml_dtypes.bfloat16)
    second = np.ascontiguousarray(first.T)
    lag = np.outer(np.arange(NB), b) % NB
    lag_cos = 2.0 * np.cos(turn * lag) / NB
    lag_cos[:, 0] = 1.0 / NB
    lag_sin = 4.0 * np.sin(turn * lag) / NB
    out_phase = lag.T
    out_sin = np.sin(turn * out_phase)
    out_sin[0] = alt
    out = np.concatenate([np.cos(turn * out_phase), out_sin]) / (NB * T_SIZE * NA)
    return first, second, pair_of(lag_cos), pair_of(lag_sin), pair_of(out)


def flip(value, mask, bits):
    out = 0
    for k in range(bits):
        unit = 2**k
        out = out + lax.rem(lax.div(value, unit) + lax.div(mask, unit), 2) * unit
    return out


def rest(x):
    return x - x.astype(jnp.bfloat16).astype(jnp.float32)


def kernel(gx_size, gy_size, v_ref, t1_ref, t2_ref, tc_ref, ts_ref, to_ref, out_ref, rv, t1, t2, tc, ts, to, even, odd, nyq,
           hbuf, hrecv, all_in, tab_sem, v_send, v_recv, h_send, h_recv):
    f32, bf16 = jnp.float32, jnp.bfloat16
    _, channels, snaps, x_rows, y_cols = v_ref.shape
    count = gx_size * gy_size
    bits = count.bit_length() - 1
    owned = channels // count
    lag_rows = NB // gx_size
    grp, gx, gy = lax.axis_index("grp"), lax.axis_index("gx"), lax.axis_index("gy")
    me = gx * gy_size + gy
    parts = snaps // T_PART

    barrier = pltpu.get_barrier_semaphore()
    quarter = gx_size // 4
    gx_bits = gx_size.bit_length() - 1
    mirror = flip(gx, 3 * quarter, gx_bits)
    inner = lax.div(lax.rem(gx + quarter, gx_size), 2 * quarter) == 1

    @pl.when(inner)
    def _():
        for oy in range(gy_size):
            pl.semaphore_signal(barrier, inc=1, device_id=(grp, mirror, oy), device_id_type=MESH)

    for k in range(2 * quarter):
        outer = (3 * quarter + k) % gx_size
        for oy in range(gy_size):

            @pl.when((outer != gx) | (oy != gy))
            def _():
                pl.semaphore_signal(barrier, inc=1, device_id=(grp, outer, oy), device_id_type=MESH)

    x_at = pl.ds(pl.multiple_of(gx * x_rows, x_rows), x_rows)
    y_at = pl.ds(pl.multiple_of(gy * y_cols, y_cols), y_cols)

    def channel_of(ox, oy, ch):
        return oy * (channels // gy_size) + ox * owned + ch

    def send_block(ox, oy, ch, part):
        times = pl.ds(part * T_PART, T_PART)
        pltpu.make_async_remote_copy(
            src_ref=v_ref.at[:, channel_of(ox, oy, ch), times],
            dst_ref=rv.at[ch, :, times, x_at, y_at],
            send_sem=v_send,
            recv_sem=v_recv.at[ch * parts + part],
            device_id=(grp, ox, oy),
            device_id_type=MESH,
        ).start()

    @pl.when(inner)
    def _():
        pl.semaphore_wait(barrier, gy_size)
        for ch in range(owned):
            for part in range(parts):
                for oy in range(gy_size):
                    send_block(mirror, oy, ch, part)

    tables = [
        pltpu.make_async_copy(src, dst, tab_sem.at[n])
        for n, (src, dst) in enumerate(((t1_ref, t1), (t2_ref, t2), (tc_ref, tc), (ts_ref, ts), (to_ref, to)))
    ]
    for copy in tables:
        copy.start()

    @pl.when(inner)
    def _():
        pl.semaphore_wait(all_in, 1)

    @pl.when(~inner)
    def _():
        pl.semaphore_wait(barrier, count - 1)
        pl.semaphore_signal(all_in, inc=1, device_id=(grp, flip(gx, quarter, gx_bits), gy), device_id_type=MESH)

    for ch in range(owned):
        for part in range(parts):
            times = pl.ds(part * T_PART, T_PART)

            def send(n, carry):
                s = lax.rem(n, 2) * (count // 2) + lax.div(n, 2)
                other = flip(me, s, bits)

                @pl.when(~inner | (lax.div(s, gy_size) != 3 * quarter))
                def _():
                    send_block(lax.div(other, gy_size), lax.rem(other, gy_size), ch, part)

                return carry

            lax.fori_loop(1, count, send, 0)
            pltpu.make_async_copy(
                v_ref.at[:, channel_of(gx, gy, ch), times], rv.at[ch, :, times, x_at, y_at], v_recv.at[ch * parts + part]
            ).start()

    for copy in tables:
        copy.wait()

    lane0 = lax.broadcasted_iota(jnp.int32, (NA, HALF), 1) == 0
    row0 = lax.broadcasted_iota(jnp.int32, (HALF, HALF), 0) == 0
    dot = functools.partial(jnp.dot, preferred_element_type=f32)

    for ch in range(owned):
        even[...] = jnp.zeros_like(even)
        odd[...] = jnp.zeros_like(odd)
        nyq[...] = jnp.zeros_like(nyq)
        for part in range(parts):
            landed = rv.at[ch, :, pl.ds(part * T_PART, T_PART)]
            pltpu.make_async_copy(landed, landed, v_recv.at[ch * parts + part]).wait()

            def snapshot(t, carry):
                re = dot(rv[ch, 0, t], t1[...])
                im = dot(rv[ch, 1, t], t1[...])
                cr, sr, ci, si = re[:, :HALF], re[:, HALF:], im[:, :HALF], im[:, HALF:]
                halves = (
                    (cr + jnp.where(lane0, 0.0, si), ci - jnp.where(lane0, 0.0, sr)),
                    (jnp.where(lane0, sr, cr - si), jnp.where(lane0, si, ci + sr)),
                )
                for n, (b_re, b_im) in enumerate(halves):
                    at = slice(n * HALF, (n + 1) * HALF)
                    re = dot(t2[...], b_re.astype(bf16))
                    im = dot(t2[...], b_im.astype(bf16))
                    cr, sr, ci, si = re[:HALF], re[HALF:], im[:HALF], im[HALF:]
                    nyq[:, at] += sr[:8] * sr[:8] + si[:8] * si[:8]
                    sr, si = jnp.where(row0, 0.0, sr), jnp.where(row0, 0.0, si)
                    even[:, at] += (cr * cr + ci * ci) + (sr * sr + si * si)
                    odd[:, at] += cr * si - ci * sr
                return carry

            lax.fori_loop(part * T_PART, (part + 1) * T_PART, snapshot, 0)

        e_hi = even[...].astype(bf16)
        e_lo = (even[...] - e_hi.astype(f32)).astype(bf16)
        o_hi = odd[...].astype(bf16)
        o_lo = (odd[...] - o_hi.astype(f32)).astype(bf16)
        alt = 1.0 - 2.0 * lax.rem(lax.broadcasted_iota(jnp.int32, (HALF, 1), 0), 2).astype(f32)
        top = nyq[0:1, :] * (1.0 / NB)
        mask = lax.broadcasted_iota(jnp.int32, (HALF, HALF), 1) == 0
        for n in range(2):
            rows = slice(n * HALF, (n + 1) * HALF)
            h_re = dot(tc[0, rows], e_hi) + dot(tc[0, rows], e_lo) + dot(tc[1, rows], e_hi) + alt * top
            h_im = dot(ts[0, rows], o_hi) + dot(ts[0, rows], o_lo) + dot(ts[1, rows], o_hi)
            rp, rm, ip, im = h_re[:, :HALF], h_re[:, HALF:], h_im[:, :HALF], h_im[:, HALF:]
            slots = [
                jnp.where(mask, rp, rp + rm),
                jnp.where(mask, rm, im - ip),
                jnp.where(mask, ip, ip + im),
                jnp.where(mask, im, rp - rm),
            ]
            if n == 0:
                slots[1] = jnp.where(row0 & ~mask, rest(rp - rm), slots[1])
                slots[2] = jnp.where(row0, rest(slots[0]), slots[2])
                slots[3] = jnp.where(row0 & mask, rest(rm), slots[3])
            for k, slot in enumerate(slots):
                hbuf[ch, rows, k * HALF : (k + 1) * HALF] = slot.astype(bf16)

        def send_lags(n, carry):
            s = lax.rem(n, 2) * (gx_size // 2) + lax.div(n, 2)
            other = flip(gx, s, gx_size.bit_length() - 1)
            pltpu.make_async_remote_copy(
                src_ref=hbuf.at[ch, pl.ds(pl.multiple_of(other * lag_rows, lag_rows), lag_rows)],
                dst_ref=hrecv.at[ch, gx],
                send_sem=h_send.at[ch],
                recv_sem=h_recv.at[ch, lax.div(gx, GROUP)],
                device_id=(grp, other, gy),
                device_id_type=MESH,
            ).start()
            return carry

        lax.fori_loop(1, gx_size, send_lags, 0)
        pltpu.make_async_copy(
            hbuf.at[ch, pl.ds(pl.multiple_of(gx * lag_rows, lag_rows), lag_rows)], hrecv.at[ch, gx], h_recv.at[ch, lax.div(gx, GROUP)]
        ).start()

    own_group = lax.div(gx, GROUP)
    zero = jnp.zeros((gx_size, HALF), bf16)
    left = lax.broadcasted_iota(jnp.int32, (gx_size, HALF), 1) == 0

    for ch in range(owned):

        def finish(n, carry):
            group = flip(own_group, n, (gx_size // GROUP).bit_length() - 1)
            sources = pl.ds(group * GROUP, GROUP)
            landed = hrecv.at[ch, sources]
            pltpu.make_async_copy(landed, landed, h_recv.at[ch, group]).wait()
            for part in range(2):
                x = hrecv[ch, sources, :, part * NB : (part + 1) * NB].reshape(GROUP * lag_rows, NB)
                y = dot(x, to[0]) + dot(x, to[1])
                out_ref[part, sources, ch] = y.reshape(GROUP, lag_rows, NB)
            return carry

        lax.fori_loop(0, gx_size // GROUP, finish, 0)

        @pl.when(gx == 0)
        def _():
            row = hrecv[ch, :, 0, :]
            a_hi, s1, a_lo, s3 = (row[:, k * HALF : (k + 1) * HALF] for k in range(4))
            for part in range(2):
                total = 0.0
                for a, b in ((a_hi, s1), (a_lo, s3)):
                    x = [a, jnp.where(left, b, zero)] if part == 0 else [zero, jnp.where(left, zero, b)]
                    x = jnp.concatenate(x, axis=1)
                    total += dot(x, to[0]) + dot(x, to[1])
                out_ref[part, :, ch, 0, :] = total

    for ch in range(owned):
        sent = hbuf.at[ch, pl.ds(0, (gx_size - 1) * lag_rows)]
        pltpu.make_async_copy(sent, sent, h_send.at[ch]).wait()
    sent = v_ref.at[:, pl.ds(0, channels - owned)]
    pltpu.make_async_copy(sent, sent, v_send).wait()


def fused(gx_size, gy_size, voltages):
    _, channels, snaps, _, _ = voltages.shape
    owned = channels // (gx_size * gy_size)
    lag_rows = NB // gx_size
    tables = [jnp.asarray(table) for table in fixed_tables()]
    bf16, f32 = jnp.bfloat16, jnp.float32
    dma = pltpu.SemaphoreType.DMA
    out = pl.pallas_call(
        functools.partial(kernel, gx_size, gy_size),
        out_shape=pltpu.VMEM((2, gx_size, owned, lag_rows, NB), f32),
        in_specs=[pl.BlockSpec(memory_space=pltpu.HBM)] * 6,
        out_specs=pl.BlockSpec(memory_space=pltpu.VMEM),
        scratch_shapes=[
            pltpu.VMEM((owned, 2, snaps, NA, NA), bf16),
            *[pltpu.VMEM(table.shape, bf16) for table in tables],
            pltpu.VMEM((HALF, NB), f32),
            pltpu.VMEM((HALF, NB), f32),
            pltpu.VMEM((8, NB), f32),
            pltpu.VMEM((owned, NB, 2 * NB), bf16),
            pltpu.VMEM((owned, gx_size, lag_rows, 2 * NB), bf16),
            pltpu.SemaphoreType.REGULAR,
            dma((5,)),
            dma,
            dma((owned * snaps // T_PART,)),
            dma((owned,)),
            dma((owned, gx_size // GROUP)),
        ],
        compiler_params=pltpu.CompilerParams(
            collective_id=0, has_side_effects=True, vmem_limit_bytes=40 * 2**20
        ),
        cost_estimate=pl.CostEstimate(flops=2 * 10**10, bytes_accessed=12 * 2**20, transcendentals=0),
    )(*[pltpu.with_memory_space_constraint(x, pltpu.HBM) for x in (voltages, *tables)])
    return out.reshape(2, gx_size * owned, lag_rows, NB)


def local(gx_size, gy_size, voltages):
    _, channels, snaps, x_rows, y_cols = voltages.shape
    count = gx_size * gy_size
    even_split = count & (count - 1) == 0 and gx_size >= 4 and gy_size == 2 and channels % count == 0
    whole_tiles = x_rows % 16 == 0 and y_cols % 128 == 0 and (NB // gx_size) % 16 == 0 and snaps % T_PART == 0
    if even_split and whole_tiles:
        return fused(gx_size, gy_size, voltages)
    return plain(voltages)


def solution(mesh):
    return jax.shard_map(
        functools.partial(local, mesh.shape["gx"], mesh.shape["gy"]),
        mesh=mesh,
        in_specs=(P(None, "grp", None, "gx", "gy"),),
        out_specs=P(None, ("grp", "gy"), "gx", None),
        check_vma=False,
    )
```

```python
import functools
import math

import jax
import jax.numpy as jnp
import ml_dtypes
import numpy as np
from jax import lax
from jax.experimental import pallas as pl
from jax.experimental.pallas import tpu as pltpu
from jax.sharding import PartitionSpec as P

NA = 256
T_SIZE = 8
NB = 512


def dft_table(row_count, col_count, sign_factor, scale_factor, out_type):
    row_index = lax.iota(jnp.int32, row_count)[:, None]
    col_index = lax.iota(jnp.int32, col_count)[None, :]
    phase_index = row_index * col_index % NB
    angles = 2.0 * math.pi / NB * phase_index.astype(jnp.float32)
    return (
        (jnp.cos(angles) * scale_factor).astype(out_type),
        (sign_factor * jnp.sin(angles) * scale_factor).astype(out_type),
    )


def plain(voltages):
    high = lax.Precision.HIGHEST
    f32 = jnp.float32
    fwd_re, fwd_im = dft_table(NA, NB, -1.0, 1.0, jnp.bfloat16)
    inv_re, inv_im = dft_table(NB, NB, 1.0, 1.0 / NB, jnp.float32)
    out_re, out_im = dft_table(NB, NB, 1.0, 1.0 / (NB * T_SIZE * NA), jnp.float32)
    turned = lax.all_to_all(voltages, "gy", split_axis=1, concat_axis=4, tiled=True)
    stacks, channels, snapshots, x_rows, y_cols = turned.shape
    gx_size = lax.axis_size("gx")
    item_count = channels * snapshots // gx_size
    group_snaps = min(item_count, snapshots)
    group_count = item_count // group_snaps
    item_rows = turned.reshape(2, channels * snapshots, x_rows, y_cols)
    received = lax.all_to_all(item_rows, "gx", split_axis=1, concat_axis=2, tiled=True)
    received = received.reshape(2, group_count, group_snaps, NA, NA)
    beam_re = jnp.einsum(
        "gtxy,yv->gtxv", received[0], fwd_re, preferred_element_type=f32
    ) - jnp.einsum("gtxy,yv->gtxv", received[1], fwd_im, preferred_element_type=f32)
    beam_im = jnp.einsum(
        "gtxy,yv->gtxv", received[0], fwd_im, preferred_element_type=f32
    ) + jnp.einsum("gtxy,yv->gtxv", received[1], fwd_re, preferred_element_type=f32)
    beam_re = beam_re.astype(jnp.bfloat16)
    beam_im = beam_im.astype(jnp.bfloat16)
    full_re = jnp.einsum("gtxv,xu->gtuv", beam_re, fwd_re, preferred_element_type=f32) - jnp.einsum(
        "gtxv,xu->gtuv", beam_im, fwd_im, preferred_element_type=f32
    )
    full_im = jnp.einsum("gtxv,xu->gtuv", beam_re, fwd_im, preferred_element_type=f32) + jnp.einsum(
        "gtxv,xu->gtuv", beam_im, fwd_re, preferred_element_type=f32
    )
    power = jnp.sum(full_re * full_re + full_im * full_im, axis=1)
    per_channel = gx_size * group_count // channels
    lag_re = jnp.einsum("guv,ul->glv", power, inv_re, precision=high)
    lag_im = jnp.einsum("guv,ul->glv", power, inv_im, precision=high)
    partial_value = jnp.stack([lag_re, lag_im], axis=1)[None]
    gathered_lags = lax.all_to_all(partial_value, "gx", split_axis=3, concat_axis=0, tiled=True)
    lag_rows_dev = gathered_lags.shape[3]
    lag_sums = jnp.sum(gathered_lags.reshape(channels, per_channel, 2, lag_rows_dev, NB), axis=1)
    vis_re = jnp.einsum("clv,vm->clm", lag_sums[:, 0], out_re, precision=high) - jnp.einsum(
        "clv,vm->clm", lag_sums[:, 1], out_im, precision=high
    )
    vis_im = jnp.einsum("clv,vm->clm", lag_sums[:, 0], out_im, precision=high) + jnp.einsum(
        "clv,vm->clm", lag_sums[:, 1], out_re, precision=high
    )
    return jnp.stack([vis_re, vis_im])


HALF = NB // 2
MESH = pl.DeviceIdType.MESH
T_PART = 4
GROUP = 4


def pair_of(x):
    high = x.astype(ml_dtypes.bfloat16)
    return np.stack([high, (x - high.astype(np.float64)).astype(ml_dtypes.bfloat16)])


def fixed_tables():
    turn = 2.0 * np.pi / NB
    a, b = np.arange(NA), np.arange(HALF)
    cos = np.cos(turn * (np.outer(a, b) % NB))
    sin = np.sin(turn * (np.outer(a, b) % NB))
    alt = 1.0 - 2.0 * (np.arange(NB) % 2)
    sin[:, 0] = alt[:NA]
    first = np.concatenate([cos, sin], axis=1).astype(ml_dtypes.bfloat16)
    second = np.ascontiguousarray(first.T)
    lag = np.outer(np.arange(NB), b) % NB
    lag_cos = 2.0 * np.cos(turn * lag) / NB
    lag_cos[:, 0] = 1.0 / NB
    lag_sin = 4.0 * np.sin(turn * lag) / NB
    out_phase = lag.T
    out_sin = np.sin(turn * out_phase)
    out_sin[0] = alt
    out = np.concatenate([np.cos(turn * out_phase), out_sin]) / (NB * T_SIZE * NA)
    return first, second, pair_of(lag_cos), pair_of(lag_sin), pair_of(out)


def flip(value, mask, bits):
    out = 0
    for k in range(bits):
        unit = 2**k
        out = out + lax.rem(lax.div(value, unit) + lax.div(mask, unit), 2) * unit
    return out


def rest(x):
    return x - x.astype(jnp.bfloat16).astype(jnp.float32)


def kernel(gx_size, gy_size, v_ref, t1_ref, t2_ref, tc_ref, ts_ref, to_ref, out_ref, rv, t1, t2, tc, ts, to, even, odd, nyq,
           hbuf, hrecv, all_in, tab_sem, v_send, v_recv, h_send, h_recv):
    f32, bf16 = jnp.float32, jnp.bfloat16
    _, channels, snaps, x_rows, y_cols = v_ref.shape
    count = gx_size * gy_size
    bits = count.bit_length() - 1
    owned = channels // count
    lag_rows = NB // gx_size
    grp, gx, gy = lax.axis_index("grp"), lax.axis_index("gx"), lax.axis_index("gy")
    me = gx * gy_size + gy
    parts = snaps // T_PART

    barrier = pltpu.get_barrier_semaphore()
    quarter = gx_size // 4
    gx_bits = gx_size.bit_length() - 1
    mirror = flip(gx, 3 * quarter, gx_bits)
    inner = lax.div(lax.rem(gx + quarter, gx_size), 2 * quarter) == 1

    @pl.when(inner)
    def _():
        for oy in range(gy_size):
            pl.semaphore_signal(barrier, inc=1, device_id=(grp, mirror, oy), device_id_type=MESH)

    for k in range(2 * quarter):
        outer = (3 * quarter + k) % gx_size
        for oy in range(gy_size):

            @pl.when((outer != gx) | (oy != gy))
            def _():
                pl.semaphore_signal(barrier, inc=1, device_id=(grp, outer, oy), device_id_type=MESH)

    x_at = pl.ds(pl.multiple_of(gx * x_rows, x_rows), x_rows)
    y_at = pl.ds(pl.multiple_of(gy * y_cols, y_cols), y_cols)

    def channel_of(ox, oy, ch):
        return oy * (channels // gy_size) + ox * owned + ch

    def send_block(ox, oy, ch, part):
        times = pl.ds(part * T_PART, T_PART)
        pltpu.make_async_remote_copy(
            src_ref=v_ref.at[:, channel_of(ox, oy, ch), times],
            dst_ref=rv.at[ch, :, times, x_at, y_at],
            send_sem=v_send,
            recv_sem=v_recv.at[ch * parts + part],
            device_id=(grp, ox, oy),
            device_id_type=MESH,
        ).start()

    @pl.when(inner)
    def _():
        pl.semaphore_wait(barrier, gy_size)
        for ch in range(owned):
            for part in range(parts):
                for oy in range(gy_size):
                    send_block(mirror, oy, ch, part)

    tables = [
        pltpu.make_async_copy(src, dst, tab_sem.at[n])
        for n, (src, dst) in enumerate(((t1_ref, t1), (t2_ref, t2), (tc_ref, tc), (ts_ref, ts), (to_ref, to)))
    ]
    for copy in tables:
        copy.start()

    @pl.when(inner)
    def _():
        pl.semaphore_wait(all_in, 1)

    @pl.when(~inner)
    def _():
        pl.semaphore_wait(barrier, count - 1)
        pl.semaphore_signal(all_in, inc=1, device_id=(grp, flip(gx, quarter, gx_bits), gy), device_id_type=MESH)

    for ch in range(owned):
        for part in range(parts):
            times = pl.ds(part * T_PART, T_PART)

            def send(n, carry):
                s = lax.rem(n, 2) * (count // 2) + lax.div(n, 2)
                other = flip(me, s, bits)

                @pl.when(~inner | (lax.div(s, gy_size) != 3 * quarter))
                def _():
                    send_block(lax.div(other, gy_size), lax.rem(other, gy_size), ch, part)

                return carry

            lax.fori_loop(1, count, send, 0)
            pltpu.make_async_copy(
                v_ref.at[:, channel_of(gx, gy, ch), times], rv.at[ch, :, times, x_at, y_at], v_recv.at[ch * parts + part]
            ).start()

    for copy in tables:
        copy.wait()

    lane0 = lax.broadcasted_iota(jnp.int32, (NA, HALF), 1) == 0
    row0 = lax.broadcasted_iota(jnp.int32, (HALF, HALF), 0) == 0
    dot = functools.partial(jnp.dot, preferred_element_type=f32)

    for ch in range(owned):
        even[...] = jnp.zeros_like(even)
        odd[...] = jnp.zeros_like(odd)
        nyq[...] = jnp.zeros_like(nyq)
        for part in range(parts):
            landed = rv.at[ch, :, pl.ds(part * T_PART, T_PART)]
            pltpu.make_async_copy(landed, landed, v_recv.at[ch * parts + part]).wait()

            def snapshot(t, carry):
                re = dot(rv[ch, 0, t], t1[...])
                im = dot(rv[ch, 1, t], t1[...])
                cr, sr, ci, si = re[:, :HALF], re[:, HALF:], im[:, :HALF], im[:, HALF:]
                halves = (
                    (cr + jnp.where(lane0, 0.0, si), ci - jnp.where(lane0, 0.0, sr)),
                    (jnp.where(lane0, sr, cr - si), jnp.where(lane0, si, ci + sr)),
                )
                for n, (b_re, b_im) in enumerate(halves):
                    at = slice(n * HALF, (n + 1) * HALF)
                    re = dot(t2[...], b_re.astype(bf16))
                    im = dot(t2[...], b_im.astype(bf16))
                    cr, sr, ci, si = re[:HALF], re[HALF:], im[:HALF], im[HALF:]
                    nyq[:, at] += sr[:8] * sr[:8] + si[:8] * si[:8]
                    sr, si = jnp.where(row0, 0.0, sr), jnp.where(row0, 0.0, si)
                    even[:, at] += (cr * cr + ci * ci) + (sr * sr + si * si)
                    odd[:, at] += cr * si - ci * sr
                return carry

            lax.fori_loop(part * T_PART, (part + 1) * T_PART, snapshot, 0)

        e_hi = even[...].astype(bf16)
        e_lo = (even[...] - e_hi.astype(f32)).astype(bf16)
        o_hi = odd[...].astype(bf16)
        o_lo = (odd[...] - o_hi.astype(f32)).astype(bf16)
        alt = 1.0 - 2.0 * lax.rem(lax.broadcasted_iota(jnp.int32, (HALF, 1), 0), 2).astype(f32)
        top = nyq[0:1, :] * (1.0 / NB)
        mask = lax.broadcasted_iota(jnp.int32, (HALF, HALF), 1) == 0
        for n in range(2):
            rows = slice(n * HALF, (n + 1) * HALF)
            h_re = dot(tc[0, rows], e_hi) + dot(tc[0, rows], e_lo) + dot(tc[1, rows], e_hi) + alt * top
            h_im = dot(ts[0, rows], o_hi) + dot(ts[0, rows], o_lo) + dot(ts[1, rows], o_hi)
            rp, rm, ip, im = h_re[:, :HALF], h_re[:, HALF:], h_im[:, :HALF], h_im[:, HALF:]
            slots = [
                jnp.where(mask, rp, rp + rm),
                jnp.where(mask, rm, im - ip),
                jnp.where(mask, ip, ip + im),
                jnp.where(mask, im, rp - rm),
            ]
            if n == 0:
                slots[1] = jnp.where(row0 & ~mask, rest(rp - rm), slots[1])
                slots[2] = jnp.where(row0, rest(slots[0]), slots[2])
                slots[3] = jnp.where(row0 & mask, rest(rm), slots[3])
            for k, slot in enumerate(slots):
                hbuf[ch, rows, k * HALF : (k + 1) * HALF] = slot.astype(bf16)

        def send_lags_to(other):
            pltpu.make_async_remote_copy(
                src_ref=hbuf.at[ch, pl.ds(pl.multiple_of(other * lag_rows, lag_rows), lag_rows)],
                dst_ref=hrecv.at[ch, gx],
                send_sem=h_send.at[ch],
                recv_sem=h_recv.at[ch, lax.div(gx, GROUP)],
                device_id=(grp, other, gy),
                device_id_type=MESH,
            ).start()

        def send_lags(n, carry):
            row = max(quarter // 2, 1)
            far = flip(gx, 2 * quarter + n, gx_bits)
            far = far - lax.rem(far, quarter) + lax.div(lax.rem(n, quarter), row) * row + lax.rem(far, row)
            send_lags_to(far)

            @pl.when(n > 0)
            def _():
                send_lags_to(flip(gx, n, gx_bits))

            return carry

        lax.fori_loop(0, 2 * quarter, send_lags, 0)
        pltpu.make_async_copy(
            hbuf.at[ch, pl.ds(pl.multiple_of(gx * lag_rows, lag_rows), lag_rows)], hrecv.at[ch, gx], h_recv.at[ch, lax.div(gx, GROUP)]
        ).start()

    own_group = lax.div(gx, GROUP)
    zero = jnp.zeros((gx_size, HALF), bf16)
    left = lax.broadcasted_iota(jnp.int32, (gx_size, HALF), 1) == 0

    for ch in range(owned):

        def finish(n, carry):
            group = flip(own_group, n, (gx_size // GROUP).bit_length() - 1)
            sources = pl.ds(group * GROUP, GROUP)
            landed = hrecv.at[ch, sources]
            pltpu.make_async_copy(landed, landed, h_recv.at[ch, group]).wait()
            for part in range(2):
                x = hrecv[ch, sources, :, part * NB : (part + 1) * NB].reshape(GROUP * lag_rows, NB)
                y = dot(x, to[0]) + dot(x, to[1])
                out_ref[part, sources, ch] = y.reshape(GROUP, lag_rows, NB)
            return carry

        lax.fori_loop(0, gx_size // GROUP, finish, 0)

        @pl.when(gx == 0)
        def _():
            row = hrecv[ch, :, 0, :]
            a_hi, s1, a_lo, s3 = (row[:, k * HALF : (k + 1) * HALF] for k in range(4))
            for part in range(2):
                total = 0.0
                for a, b in ((a_hi, s1), (a_lo, s3)):
                    x = [a, jnp.where(left, b, zero)] if part == 0 else [zero, jnp.where(left, zero, b)]
                    x = jnp.concatenate(x, axis=1)
                    total += dot(x, to[0]) + dot(x, to[1])
                out_ref[part, :, ch, 0, :] = total

    for ch in range(owned):
        sent = hbuf.at[ch, pl.ds(0, (gx_size - 1) * lag_rows)]
        pltpu.make_async_copy(sent, sent, h_send.at[ch]).wait()
    sent = v_ref.at[:, pl.ds(0, channels - owned)]
    pltpu.make_async_copy(sent, sent, v_send).wait()


def fused(gx_size, gy_size, voltages):
    _, channels, snaps, _, _ = voltages.shape
    owned = channels // (gx_size * gy_size)
    lag_rows = NB // gx_size
    tables = [jnp.asarray(table) for table in fixed_tables()]
    bf16, f32 = jnp.bfloat16, jnp.float32
    dma = pltpu.SemaphoreType.DMA
    out = pl.pallas_call(
        functools.partial(kernel, gx_size, gy_size),
        out_shape=pltpu.VMEM((2, gx_size, owned, lag_rows, NB), f32),
        in_specs=[pl.BlockSpec(memory_space=pltpu.HBM)] * 6,
        out_specs=pl.BlockSpec(memory_space=pltpu.VMEM),
        scratch_shapes=[
            pltpu.VMEM((owned, 2, snaps, NA, NA), bf16),
            *[pltpu.VMEM(table.shape, bf16) for table in tables],
            pltpu.VMEM((HALF, NB), f32),
            pltpu.VMEM((HALF, NB), f32),
            pltpu.VMEM((8, NB), f32),
            pltpu.VMEM((owned, NB, 2 * NB), bf16),
            pltpu.VMEM((owned, gx_size, lag_rows, 2 * NB), bf16),
            pltpu.SemaphoreType.REGULAR,
            dma((5,)),
            dma,
            dma((owned * snaps // T_PART,)),
            dma((owned,)),
            dma((owned, gx_size // GROUP)),
        ],
        compiler_params=pltpu.CompilerParams(
            collective_id=0, has_side_effects=True, vmem_limit_bytes=40 * 2**20
        ),
        cost_estimate=pl.CostEstimate(flops=2 * 10**10, bytes_accessed=12 * 2**20, transcendentals=0),
    )(*[pltpu.with_memory_space_constraint(x, pltpu.HBM) for x in (voltages, *tables)])
    return out.reshape(2, gx_size * owned, lag_rows, NB)


def local(gx_size, gy_size, voltages):
    _, channels, snaps, x_rows, y_cols = voltages.shape
    count = gx_size * gy_size
    even_split = count & (count - 1) == 0 and gx_size >= 4 and gy_size == 2 and channels % count == 0
    whole_tiles = x_rows % 16 == 0 and y_cols % 128 == 0 and (NB // gx_size) % 16 == 0 and snaps % T_PART == 0
    if even_split and whole_tiles:
        return fused(gx_size, gy_size, voltages)
    return plain(voltages)


def solution(mesh):
    return jax.shard_map(
        functools.partial(local, mesh.shape["gx"], mesh.shape["gy"]),
        mesh=mesh,
        in_specs=(P(None, "grp", None, "gx", "gy"),),
        out_specs=P(None, ("grp", "gy"), "gx", None),
        check_vma=False,
    )
```

```python
import functools
import math

import jax
import jax.numpy as jnp
import ml_dtypes
import numpy as np
from jax import lax
from jax.experimental import pallas as pl
from jax.experimental.pallas import tpu as pltpu
from jax.sharding import PartitionSpec as P

NA = 256
T_SIZE = 8
NB = 512


def dft_table(row_count, col_count, sign_factor, scale_factor, out_type):
    row_index = lax.iota(jnp.int32, row_count)[:, None]
    col_index = lax.iota(jnp.int32, col_count)[None, :]
    phase_index = row_index * col_index % NB
    angles = 2.0 * math.pi / NB * phase_index.astype(jnp.float32)
    return (
        (jnp.cos(angles) * scale_factor).astype(out_type),
        (sign_factor * jnp.sin(angles) * scale_factor).astype(out_type),
    )


def plain(voltages):
    high = lax.Precision.HIGHEST
    f32 = jnp.float32
    fwd_re, fwd_im = dft_table(NA, NB, -1.0, 1.0, jnp.bfloat16)
    inv_re, inv_im = dft_table(NB, NB, 1.0, 1.0 / NB, jnp.float32)
    out_re, out_im = dft_table(NB, NB, 1.0, 1.0 / (NB * T_SIZE * NA), jnp.float32)
    turned = lax.all_to_all(voltages, "gy", split_axis=1, concat_axis=4, tiled=True)
    stacks, channels, snapshots, x_rows, y_cols = turned.shape
    gx_size = lax.axis_size("gx")
    item_count = channels * snapshots // gx_size
    group_snaps = min(item_count, snapshots)
    group_count = item_count // group_snaps
    item_rows = turned.reshape(2, channels * snapshots, x_rows, y_cols)
    received = lax.all_to_all(item_rows, "gx", split_axis=1, concat_axis=2, tiled=True)
    received = received.reshape(2, group_count, group_snaps, NA, NA)
    beam_re = jnp.einsum(
        "gtxy,yv->gtxv", received[0], fwd_re, preferred_element_type=f32
    ) - jnp.einsum("gtxy,yv->gtxv", received[1], fwd_im, preferred_element_type=f32)
    beam_im = jnp.einsum(
        "gtxy,yv->gtxv", received[0], fwd_im, preferred_element_type=f32
    ) + jnp.einsum("gtxy,yv->gtxv", received[1], fwd_re, preferred_element_type=f32)
    beam_re = beam_re.astype(jnp.bfloat16)
    beam_im = beam_im.astype(jnp.bfloat16)
    full_re = jnp.einsum("gtxv,xu->gtuv", beam_re, fwd_re, preferred_element_type=f32) - jnp.einsum(
        "gtxv,xu->gtuv", beam_im, fwd_im, preferred_element_type=f32
    )
    full_im = jnp.einsum("gtxv,xu->gtuv", beam_re, fwd_im, preferred_element_type=f32) + jnp.einsum(
        "gtxv,xu->gtuv", beam_im, fwd_re, preferred_element_type=f32
    )
    power = jnp.sum(full_re * full_re + full_im * full_im, axis=1)
    per_channel = gx_size * group_count // channels
    lag_re = jnp.einsum("guv,ul->glv", power, inv_re, precision=high)
    lag_im = jnp.einsum("guv,ul->glv", power, inv_im, precision=high)
    partial_value = jnp.stack([lag_re, lag_im], axis=1)[None]
    gathered_lags = lax.all_to_all(partial_value, "gx", split_axis=3, concat_axis=0, tiled=True)
    lag_rows_dev = gathered_lags.shape[3]
    lag_sums = jnp.sum(gathered_lags.reshape(channels, per_channel, 2, lag_rows_dev, NB), axis=1)
    vis_re = jnp.einsum("clv,vm->clm", lag_sums[:, 0], out_re, precision=high) - jnp.einsum(
        "clv,vm->clm", lag_sums[:, 1], out_im, precision=high
    )
    vis_im = jnp.einsum("clv,vm->clm", lag_sums[:, 0], out_im, precision=high) + jnp.einsum(
        "clv,vm->clm", lag_sums[:, 1], out_re, precision=high
    )
    return jnp.stack([vis_re, vis_im])


HALF = NB // 2
MESH = pl.DeviceIdType.MESH
T_PART = 4
GROUP = 4


def pair_of(x):
    high = x.astype(ml_dtypes.bfloat16)
    return np.stack([high, (x - high.astype(np.float64)).astype(ml_dtypes.bfloat16)])


def fixed_tables():
    turn = 2.0 * np.pi / NB
    a, b = np.arange(NA), np.arange(HALF)
    cos = np.cos(turn * (np.outer(a, b) % NB))
    sin = np.sin(turn * (np.outer(a, b) % NB))
    alt = 1.0 - 2.0 * (np.arange(NB) % 2)
    sin[:, 0] = alt[:NA]
    first = np.concatenate([cos, sin], axis=1).astype(ml_dtypes.bfloat16)
    second = np.ascontiguousarray(first.T)
    lag = np.outer(np.arange(NB), b) % NB
    lag_cos = 2.0 * np.cos(turn * lag) / NB
    lag_cos[:, 0] = 1.0 / NB
    lag_sin = 4.0 * np.sin(turn * lag) / NB
    out_phase = lag.T
    out_sin = np.sin(turn * out_phase)
    out_sin[0] = alt
    out = np.concatenate([np.cos(turn * out_phase), out_sin]) / (NB * T_SIZE * NA)
    return first, second, pair_of(lag_cos), pair_of(lag_sin), pair_of(out)


def flip(value, mask, bits):
    out = 0
    for k in range(bits):
        unit = 2**k
        out = out + lax.rem(lax.div(value, unit) + lax.div(mask, unit), 2) * unit
    return out


def rest(x):
    return x - x.astype(jnp.bfloat16).astype(jnp.float32)


def kernel(gx_size, gy_size, v_ref, t1_ref, t2_ref, tc_ref, ts_ref, to_ref, out_ref, rv, t1, t2, tc, ts, to, even, odd, nyq,
           hbuf, hrecv, all_in, tab_sem, v_send, v_recv, h_send, h_recv):
    f32, bf16 = jnp.float32, jnp.bfloat16
    _, channels, snaps, x_rows, y_cols = v_ref.shape
    count = gx_size * gy_size
    bits = count.bit_length() - 1
    owned = channels // count
    lag_rows = NB // gx_size
    grp, gx, gy = lax.axis_index("grp"), lax.axis_index("gx"), lax.axis_index("gy")
    me = gx * gy_size + gy
    parts = snaps // T_PART

    barrier = pltpu.get_barrier_semaphore()
    quarter = gx_size // 4
    gx_bits = gx_size.bit_length() - 1
    mirror = flip(gx, 3 * quarter, gx_bits)
    inner = lax.div(lax.rem(gx + quarter, gx_size), 2 * quarter) == 1

    @pl.when(inner)
    def _():
        for oy in range(gy_size):

            @pl.when(oy <= gy)
            def _():
                pl.semaphore_signal(barrier, inc=1, device_id=(grp, mirror, oy), device_id_type=MESH)


    for k in range(2 * quarter):
        outer = (3 * quarter + k) % gx_size
        for oy in range(gy_size):

            @pl.when((outer != gx) | (oy != gy))
            def _():
                pl.semaphore_signal(barrier, inc=1, device_id=(grp, outer, oy), device_id_type=MESH)

    x_at = pl.ds(pl.multiple_of(gx * x_rows, x_rows), x_rows)
    y_at = pl.ds(pl.multiple_of(gy * y_cols, y_cols), y_cols)

    def channel_of(ox, oy, ch):
        return oy * (channels // gy_size) + ox * owned + ch

    def send_block(ox, oy, ch, part):
        times = pl.ds(part * T_PART, T_PART)
        pltpu.make_async_remote_copy(
            src_ref=v_ref.at[:, channel_of(ox, oy, ch), times],
            dst_ref=rv.at[ch, :, times, x_at, y_at],
            send_sem=v_send,
            recv_sem=v_recv.at[ch * parts + part],
            device_id=(grp, ox, oy),
            device_id_type=MESH,
        ).start()

    @pl.when(inner)
    def _():
        pl.semaphore_wait(barrier, gy_size - gy)
        for ch in range(owned):
            for part in range(parts):
                for oy in range(gy_size):

                    @pl.when(oy >= gy)
                    def _():
                        send_block(mirror, oy, ch, part)


    tables = [
        pltpu.make_async_copy(src, dst, tab_sem.at[n])
        for n, (src, dst) in enumerate(((t1_ref, t1), (t2_ref, t2), (tc_ref, tc), (ts_ref, ts), (to_ref, to)))
    ]
    for copy in tables:
        copy.start()

    @pl.when(inner)
    def _():
        pl.semaphore_wait(all_in, 1)

    @pl.when(~inner)
    def _():
        pl.semaphore_wait(barrier, count - 1)
        pl.semaphore_signal(all_in, inc=1, device_id=(grp, flip(gx, quarter, gx_bits), gy), device_id_type=MESH)

    for ch in range(owned):
        for part in range(parts):
            times = pl.ds(part * T_PART, T_PART)

            def send(n, carry):
                s = lax.rem(n, 2) * (count // 2) + lax.div(n, 2)
                other = flip(me, s, bits)

                @pl.when(~inner | (lax.div(s, gy_size) != 3 * quarter) | (lax.rem(other, gy_size) < gy))
                def _():
                    send_block(lax.div(other, gy_size), lax.rem(other, gy_size), ch, part)

                return carry

            lax.fori_loop(1, count, send, 0)
            pltpu.make_async_copy(
                v_ref.at[:, channel_of(gx, gy, ch), times], rv.at[ch, :, times, x_at, y_at], v_recv.at[ch * parts + part]
            ).start()

    for copy in tables:
        copy.wait()

    lane0 = lax.broadcasted_iota(jnp.int32, (NA, HALF), 1) == 0
    row0 = lax.broadcasted_iota(jnp.int32, (HALF, HALF), 0) == 0
    dot = functools.partial(jnp.dot, preferred_element_type=f32)

    for ch in range(owned):
        even[...] = jnp.zeros_like(even)
        odd[...] = jnp.zeros_like(odd)
        nyq[...] = jnp.zeros_like(nyq)
        for part in range(parts):
            landed = rv.at[ch, :, pl.ds(part * T_PART, T_PART)]
            pltpu.make_async_copy(landed, landed, v_recv.at[ch * parts + part]).wait()

            def snapshot(t, carry):
                re = dot(rv[ch, 0, t], t1[...])
                im = dot(rv[ch, 1, t], t1[...])
                cr, sr, ci, si = re[:, :HALF], re[:, HALF:], im[:, :HALF], im[:, HALF:]
                halves = (
                    (cr + jnp.where(lane0, 0.0, si), ci - jnp.where(lane0, 0.0, sr)),
                    (jnp.where(lane0, sr, cr - si), jnp.where(lane0, si, ci + sr)),
                )
                for n, (b_re, b_im) in enumerate(halves):
                    at = slice(n * HALF, (n + 1) * HALF)
                    re = dot(t2[...], b_re.astype(bf16))
                    im = dot(t2[...], b_im.astype(bf16))
                    cr, sr, ci, si = re[:HALF], re[HALF:], im[:HALF], im[HALF:]
                    nyq[:, at] += sr[:8] * sr[:8] + si[:8] * si[:8]
                    sr, si = jnp.where(row0, 0.0, sr), jnp.where(row0, 0.0, si)
                    even[:, at] += (cr * cr + ci * ci) + (sr * sr + si * si)
                    odd[:, at] += cr * si - ci * sr
                return carry

            lax.fori_loop(part * T_PART, (part + 1) * T_PART, snapshot, 0)

        e_hi = even[...].astype(bf16)
        e_lo = (even[...] - e_hi.astype(f32)).astype(bf16)
        o_hi = odd[...].astype(bf16)
        o_lo = (odd[...] - o_hi.astype(f32)).astype(bf16)
        alt = 1.0 - 2.0 * lax.rem(lax.broadcasted_iota(jnp.int32, (HALF, 1), 0), 2).astype(f32)
        top = nyq[0:1, :] * (1.0 / NB)
        mask = lax.broadcasted_iota(jnp.int32, (HALF, HALF), 1) == 0
        for n in range(2):
            rows = slice(n * HALF, (n + 1) * HALF)
            h_re = dot(tc[0, rows], e_hi) + dot(tc[0, rows], e_lo) + dot(tc[1, rows], e_hi) + alt * top
            h_im = dot(ts[0, rows], o_hi) + dot(ts[0, rows], o_lo) + dot(ts[1, rows], o_hi)
            rp, rm, ip, im = h_re[:, :HALF], h_re[:, HALF:], h_im[:, :HALF], h_im[:, HALF:]
            slots = [
                jnp.where(mask, rp, rp + rm),
                jnp.where(mask, rm, im - ip),
                jnp.where(mask, ip, ip + im),
                jnp.where(mask, im, rp - rm),
            ]
            if n == 0:
                slots[1] = jnp.where(row0 & ~mask, rest(rp - rm), slots[1])
                slots[2] = jnp.where(row0, rest(slots[0]), slots[2])
                slots[3] = jnp.where(row0 & mask, rest(rm), slots[3])
            for k, slot in enumerate(slots):
                hbuf[ch, rows, k * HALF : (k + 1) * HALF] = slot.astype(bf16)

        def send_lags_to(other):
            pltpu.make_async_remote_copy(
                src_ref=hbuf.at[ch, pl.ds(pl.multiple_of(other * lag_rows, lag_rows), lag_rows)],
                dst_ref=hrecv.at[ch, gx],
                send_sem=h_send.at[ch],
                recv_sem=h_recv.at[ch, lax.div(gx, GROUP)],
                device_id=(grp, other, gy),
                device_id_type=MESH,
            ).start()

        def send_lags(n, carry):
            row = max(quarter // 2, 1)
            far = flip(gx, 2 * quarter + n, gx_bits)
            y, k = lax.div(lax.rem(n, quarter), row), lax.rem(n, row)
            x = jnp.where((y == 0) | (lax.rem(gx, quarter) < row), lax.rem(far, row), k)
            far = far - lax.rem(far, quarter) + y * row + x
            send_lags_to(far)

            @pl.when(n > 0)
            def _():
                send_lags_to(flip(gx, n, gx_bits))

            return carry

        lax.fori_loop(0, 2 * quarter, send_lags, 0)
        pltpu.make_async_copy(
            hbuf.at[ch, pl.ds(pl.multiple_of(gx * lag_rows, lag_rows), lag_rows)], hrecv.at[ch, gx], h_recv.at[ch, lax.div(gx, GROUP)]
        ).start()

    own_group = lax.div(gx, GROUP)
    zero = jnp.zeros((gx_size, HALF), bf16)
    left = lax.broadcasted_iota(jnp.int32, (gx_size, HALF), 1) == 0

    for ch in range(owned):

        def finish(n, carry):
            group = flip(own_group, n, (gx_size // GROUP).bit_length() - 1)
            sources = pl.ds(group * GROUP, GROUP)
            landed = hrecv.at[ch, sources]
            pltpu.make_async_copy(landed, landed, h_recv.at[ch, group]).wait()
            for part in range(2):
                x = hrecv[ch, sources, :, part * NB : (part + 1) * NB].reshape(GROUP * lag_rows, NB)
                y = dot(x, to[0]) + dot(x, to[1])
                out_ref[part, sources, ch] = y.reshape(GROUP, lag_rows, NB)
            return carry

        lax.fori_loop(0, gx_size // GROUP, finish, 0)

        @pl.when(gx == 0)
        def _():
            row = hrecv[ch, :, 0, :]
            a_hi, s1, a_lo, s3 = (row[:, k * HALF : (k + 1) * HALF] for k in range(4))
            for part in range(2):
                total = 0.0
                for a, b in ((a_hi, s1), (a_lo, s3)):
                    x = [a, jnp.where(left, b, zero)] if part == 0 else [zero, jnp.where(left, zero, b)]
                    x = jnp.concatenate(x, axis=1)
                    total += dot(x, to[0]) + dot(x, to[1])
                out_ref[part, :, ch, 0, :] = total

    for ch in range(owned):
        sent = hbuf.at[ch, pl.ds(0, (gx_size - 1) * lag_rows)]
        pltpu.make_async_copy(sent, sent, h_send.at[ch]).wait()
    sent = v_ref.at[:, pl.ds(0, channels - owned)]
    pltpu.make_async_copy(sent, sent, v_send).wait()


def fused(gx_size, gy_size, voltages):
    _, channels, snaps, _, _ = voltages.shape
    owned = channels // (gx_size * gy_size)
    lag_rows = NB // gx_size
    tables = [jnp.asarray(table) for table in fixed_tables()]
    bf16, f32 = jnp.bfloat16, jnp.float32
    dma = pltpu.SemaphoreType.DMA
    out = pl.pallas_call(
        functools.partial(kernel, gx_size, gy_size),
        out_shape=pltpu.VMEM((2, gx_size, owned, lag_rows, NB), f32),
        in_specs=[pl.BlockSpec(memory_space=pltpu.HBM)] * 6,
        out_specs=pl.BlockSpec(memory_space=pltpu.VMEM),
        scratch_shapes=[
            pltpu.VMEM((owned, 2, snaps, NA, NA), bf16),
            *[pltpu.VMEM(table.shape, bf16) for table in tables],
            pltpu.VMEM((HALF, NB), f32),
            pltpu.VMEM((HALF, NB), f32),
            pltpu.VMEM((8, NB), f32),
            pltpu.VMEM((owned, NB, 2 * NB), bf16),
            pltpu.VMEM((owned, gx_size, lag_rows, 2 * NB), bf16),
            pltpu.SemaphoreType.REGULAR,
            dma((5,)),
            dma,
            dma((owned * snaps // T_PART,)),
            dma((owned,)),
            dma((owned, gx_size // GROUP)),
        ],
        compiler_params=pltpu.CompilerParams(
            collective_id=0, has_side_effects=True, vmem_limit_bytes=40 * 2**20
        ),
        cost_estimate=pl.CostEstimate(flops=2 * 10**10, bytes_accessed=12 * 2**20, transcendentals=0),
    )(*[pltpu.with_memory_space_constraint(x, pltpu.HBM) for x in (voltages, *tables)])
    return out.reshape(2, gx_size * owned, lag_rows, NB)


def local(gx_size, gy_size, voltages):
    _, channels, snaps, x_rows, y_cols = voltages.shape
    count = gx_size * gy_size
    even_split = count & (count - 1) == 0 and gx_size >= 4 and gy_size == 2 and channels % count == 0
    whole_tiles = x_rows % 16 == 0 and y_cols % 128 == 0 and (NB // gx_size) % 16 == 0 and snaps % T_PART == 0
    if even_split and whole_tiles:
        return fused(gx_size, gy_size, voltages)
    return plain(voltages)


def solution(mesh):
    return jax.shard_map(
        functools.partial(local, mesh.shape["gx"], mesh.shape["gy"]),
        mesh=mesh,
        in_specs=(P(None, "grp", None, "gx", "gy"),),
        out_specs=P(None, ("grp", "gy"), "gx", None),
        check_vma=False,
    )
```

```python
import functools
import math

import jax
import jax.numpy as jnp
import ml_dtypes
import numpy as np
from jax import lax
from jax.experimental import pallas as pl
from jax.experimental.pallas import tpu as pltpu
from jax.sharding import PartitionSpec as P

NA = 256
T_SIZE = 8
NB = 512


def dft_table(row_count, col_count, sign_factor, scale_factor, out_type):
    row_index = lax.iota(jnp.int32, row_count)[:, None]
    col_index = lax.iota(jnp.int32, col_count)[None, :]
    phase_index = row_index * col_index % NB
    angles = 2.0 * math.pi / NB * phase_index.astype(jnp.float32)
    return (
        (jnp.cos(angles) * scale_factor).astype(out_type),
        (sign_factor * jnp.sin(angles) * scale_factor).astype(out_type),
    )


def plain(voltages):
    high = lax.Precision.HIGHEST
    f32 = jnp.float32
    fwd_re, fwd_im = dft_table(NA, NB, -1.0, 1.0, jnp.bfloat16)
    inv_re, inv_im = dft_table(NB, NB, 1.0, 1.0 / NB, jnp.float32)
    out_re, out_im = dft_table(NB, NB, 1.0, 1.0 / (NB * T_SIZE * NA), jnp.float32)
    turned = lax.all_to_all(voltages, "gy", split_axis=1, concat_axis=4, tiled=True)
    stacks, channels, snapshots, x_rows, y_cols = turned.shape
    gx_size = lax.axis_size("gx")
    item_count = channels * snapshots // gx_size
    group_snaps = min(item_count, snapshots)
    group_count = item_count // group_snaps
    item_rows = turned.reshape(2, channels * snapshots, x_rows, y_cols)
    received = lax.all_to_all(item_rows, "gx", split_axis=1, concat_axis=2, tiled=True)
    received = received.reshape(2, group_count, group_snaps, NA, NA)
    beam_re = jnp.einsum(
        "gtxy,yv->gtxv", received[0], fwd_re, preferred_element_type=f32
    ) - jnp.einsum("gtxy,yv->gtxv", received[1], fwd_im, preferred_element_type=f32)
    beam_im = jnp.einsum(
        "gtxy,yv->gtxv", received[0], fwd_im, preferred_element_type=f32
    ) + jnp.einsum("gtxy,yv->gtxv", received[1], fwd_re, preferred_element_type=f32)
    beam_re = beam_re.astype(jnp.bfloat16)
    beam_im = beam_im.astype(jnp.bfloat16)
    full_re = jnp.einsum("gtxv,xu->gtuv", beam_re, fwd_re, preferred_element_type=f32) - jnp.einsum(
        "gtxv,xu->gtuv", beam_im, fwd_im, preferred_element_type=f32
    )
    full_im = jnp.einsum("gtxv,xu->gtuv", beam_re, fwd_im, preferred_element_type=f32) + jnp.einsum(
        "gtxv,xu->gtuv", beam_im, fwd_re, preferred_element_type=f32
    )
    power = jnp.sum(full_re * full_re + full_im * full_im, axis=1)
    per_channel = gx_size * group_count // channels
    lag_re = jnp.einsum("guv,ul->glv", power, inv_re, precision=high)
    lag_im = jnp.einsum("guv,ul->glv", power, inv_im, precision=high)
    partial_value = jnp.stack([lag_re, lag_im], axis=1)[None]
    gathered_lags = lax.all_to_all(partial_value, "gx", split_axis=3, concat_axis=0, tiled=True)
    lag_rows_dev = gathered_lags.shape[3]
    lag_sums = jnp.sum(gathered_lags.reshape(channels, per_channel, 2, lag_rows_dev, NB), axis=1)
    vis_re = jnp.einsum("clv,vm->clm", lag_sums[:, 0], out_re, precision=high) - jnp.einsum(
        "clv,vm->clm", lag_sums[:, 1], out_im, precision=high
    )
    vis_im = jnp.einsum("clv,vm->clm", lag_sums[:, 0], out_im, precision=high) + jnp.einsum(
        "clv,vm->clm", lag_sums[:, 1], out_re, precision=high
    )
    return jnp.stack([vis_re, vis_im])


HALF = NB // 2
MESH = pl.DeviceIdType.MESH
T_PART = 4
GROUP = 4


def pair_of(x):
    high = x.astype(ml_dtypes.bfloat16)
    return np.stack([high, (x - high.astype(np.float64)).astype(ml_dtypes.bfloat16)])


def fixed_tables():
    turn = 2.0 * np.pi / NB
    a, b = np.arange(NA), np.arange(HALF)
    cos = np.cos(turn * (np.outer(a, b) % NB))
    sin = np.sin(turn * (np.outer(a, b) % NB))
    alt = 1.0 - 2.0 * (np.arange(NB) % 2)
    sin[:, 0] = alt[:NA]
    first = np.concatenate([cos, sin], axis=1).astype(ml_dtypes.bfloat16)
    second = np.ascontiguousarray(first.T)
    lag = np.outer(np.arange(NB), b) % NB
    lag_cos = 2.0 * np.cos(turn * lag) / NB
    lag_cos[:, 0] = 1.0 / NB
    lag_sin = 4.0 * np.sin(turn * lag) / NB
    out_phase = lag.T
    out_sin = np.sin(turn * out_phase)
    out_sin[0] = alt
    out = np.concatenate([np.cos(turn * out_phase), out_sin]) / (NB * T_SIZE * NA)
    return first, second, pair_of(lag_cos), pair_of(lag_sin), pair_of(out)


def flip(value, mask, bits):
    out = 0
    for k in range(bits):
        unit = 2**k
        out = out + lax.rem(lax.div(value, unit) + lax.div(mask, unit), 2) * unit
    return out


def rest(x):
    return x - x.astype(jnp.bfloat16).astype(jnp.float32)


def kernel(gx_size, gy_size, v_ref, t1_ref, t2_ref, tc_ref, ts_ref, to_ref, out_ref, rv, t1, t2, tc, ts, to, even, odd, nyq,
           hbuf, hrecv, all_in, tab_sem, v_send, v_recv, h_send, h_recv):
    f32, bf16 = jnp.float32, jnp.bfloat16
    _, channels, snaps, x_rows, y_cols = v_ref.shape
    count = gx_size * gy_size
    bits = count.bit_length() - 1
    owned = channels // count
    lag_rows = NB // gx_size
    grp, gx, gy = lax.axis_index("grp"), lax.axis_index("gx"), lax.axis_index("gy")
    me = gx * gy_size + gy
    parts = snaps // T_PART

    barrier = pltpu.get_barrier_semaphore()
    quarter = gx_size // 4
    gx_bits = gx_size.bit_length() - 1
    mirror = flip(gx, 3 * quarter, gx_bits)
    inner = lax.div(lax.rem(gx + quarter, gx_size), 2 * quarter) == 1

    @pl.when(inner)
    def _():
        for oy in range(gy_size):

            @pl.when(oy <= gy)
            def _():
                pl.semaphore_signal(barrier, inc=1, device_id=(grp, mirror, oy), device_id_type=MESH)

    for k in range(2 * quarter):
        outer = (3 * quarter + k) % gx_size
        for oy in range(gy_size):

            @pl.when((outer != gx) | (oy != gy))
            def _():
                pl.semaphore_signal(barrier, inc=1, device_id=(grp, outer, oy), device_id_type=MESH)

    x_at = pl.ds(pl.multiple_of(gx * x_rows, x_rows), x_rows)
    y_at = pl.ds(pl.multiple_of(gy * y_cols, y_cols), y_cols)

    def channel_of(ox, oy, ch):
        return oy * (channels // gy_size) + ox * owned + ch

    def send_block(ox, oy, ch, part):
        times = pl.ds(part * T_PART, T_PART)
        pltpu.make_async_remote_copy(
            src_ref=v_ref.at[:, channel_of(ox, oy, ch), times],
            dst_ref=rv.at[ch, :, times, x_at, y_at],
            send_sem=v_send,
            recv_sem=v_recv.at[ch * parts + part],
            device_id=(grp, ox, oy),
            device_id_type=MESH,
        ).start()

    @pl.when(inner)
    def _():
        pl.semaphore_wait(barrier, gy_size - gy)
        for ch in range(owned):
            for part in range(parts):
                for oy in range(gy_size):

                    @pl.when(oy >= gy)
                    def _():
                        send_block(mirror, oy, ch, part)

    tables = [
        pltpu.make_async_copy(src, dst, tab_sem.at[n])
        for n, (src, dst) in enumerate(((t1_ref, t1), (t2_ref, t2), (tc_ref, tc), (ts_ref, ts), (to_ref, to)))
    ]
    for copy in tables:
        copy.start()

    @pl.when(inner)
    def _():
        pl.semaphore_wait(all_in, 1)

    @pl.when(~inner)
    def _():
        pl.semaphore_wait(barrier, count - 1)
        pl.semaphore_signal(all_in, inc=1, device_id=(grp, flip(gx, quarter, gx_bits), gy), device_id_type=MESH)

    for ch in range(owned):
        for part in range(parts):
            times = pl.ds(part * T_PART, T_PART)

            def send(n, carry):
                s = lax.rem(n, 2) * (count // 2) + lax.div(n, 2)
                other = flip(me, s, bits)

                @pl.when(~inner | (lax.div(s, gy_size) != 3 * quarter) | (lax.rem(other, gy_size) < gy))
                def _():
                    send_block(lax.div(other, gy_size), lax.rem(other, gy_size), ch, part)

                return carry

            lax.fori_loop(1, count, send, 0)
            pltpu.make_async_copy(
                v_ref.at[:, channel_of(gx, gy, ch), times], rv.at[ch, :, times, x_at, y_at], v_recv.at[ch * parts + part]
            ).start()

    for copy in tables:
        copy.wait()

    lane0 = lax.broadcasted_iota(jnp.int32, (NA, HALF), 1) == 0
    row0 = lax.broadcasted_iota(jnp.int32, (HALF, HALF), 0) == 0
    dot = functools.partial(jnp.dot, preferred_element_type=f32)

    for ch in range(owned):
        even[...] = jnp.zeros_like(even)
        odd[...] = jnp.zeros_like(odd)
        nyq[...] = jnp.zeros_like(nyq)
        for part in range(parts):
            landed = rv.at[ch, :, pl.ds(part * T_PART, T_PART)]
            pltpu.make_async_copy(landed, landed, v_recv.at[ch * parts + part]).wait()

            def snapshot(t, carry):
                re = dot(rv[ch, 0, t], t1[...])
                im = dot(rv[ch, 1, t], t1[...])
                cr, sr, ci, si = re[:, :HALF], re[:, HALF:], im[:, :HALF], im[:, HALF:]
                halves = (
                    (cr + jnp.where(lane0, 0.0, si), ci - jnp.where(lane0, 0.0, sr)),
                    (jnp.where(lane0, sr, cr - si), jnp.where(lane0, si, ci + sr)),
                )
                for n, (b_re, b_im) in enumerate(halves):
                    at = slice(n * HALF, (n + 1) * HALF)
                    re = dot(t2[...], b_re.astype(bf16))
                    im = dot(t2[...], b_im.astype(bf16))
                    cr, sr, ci, si = re[:HALF], re[HALF:], im[:HALF], im[HALF:]
                    nyq[:, at] += sr[:8] * sr[:8] + si[:8] * si[:8]
                    sr, si = jnp.where(row0, 0.0, sr), jnp.where(row0, 0.0, si)
                    even[:, at] += (cr * cr + ci * ci) + (sr * sr + si * si)
                    odd[:, at] += cr * si - ci * sr
                return carry

            lax.fori_loop(part * T_PART, (part + 1) * T_PART, snapshot, 0)

        e_hi = even[...].astype(bf16)
        e_lo = (even[...] - e_hi.astype(f32)).astype(bf16)
        o_hi = odd[...].astype(bf16)
        o_lo = (odd[...] - o_hi.astype(f32)).astype(bf16)
        alt = 1.0 - 2.0 * lax.rem(lax.broadcasted_iota(jnp.int32, (HALF, 1), 0), 2).astype(f32)
        top = nyq[0:1, :] * (1.0 / NB)
        mask = lax.broadcasted_iota(jnp.int32, (HALF, HALF), 1) == 0
        for n in range(2):
            rows = slice(n * HALF, (n + 1) * HALF)
            h_re = dot(tc[0, rows], e_hi) + dot(tc[0, rows], e_lo) + dot(tc[1, rows], e_hi) + alt * top
            h_im = dot(ts[0, rows], o_hi) + dot(ts[0, rows], o_lo) + dot(ts[1, rows], o_hi)
            rp, rm, ip, im = h_re[:, :HALF], h_re[:, HALF:], h_im[:, :HALF], h_im[:, HALF:]
            slots = [
                jnp.where(mask, rp, rp + rm),
                jnp.where(mask, rm, im - ip),
                jnp.where(mask, ip, ip + im),
                jnp.where(mask, im, rp - rm),
            ]
            if n == 0:
                slots[1] = jnp.where(row0 & ~mask, rest(rp - rm), slots[1])
                slots[2] = jnp.where(row0, rest(slots[0]), slots[2])
                slots[3] = jnp.where(row0 & mask, rest(rm), slots[3])
            for k, slot in enumerate(slots):
                hbuf[ch, rows, k * HALF : (k + 1) * HALF] = slot.astype(bf16)

        def send_lags_to(other):
            pltpu.make_async_remote_copy(
                src_ref=hbuf.at[ch, pl.ds(pl.multiple_of(other * lag_rows, lag_rows), lag_rows)],
                dst_ref=hrecv.at[ch, gx],
                send_sem=h_send.at[ch],
                recv_sem=h_recv.at[ch, lax.div(gx, GROUP)],
                device_id=(grp, other, gy),
                device_id_type=MESH,
            ).start()

        def send_lags(n, carry):
            row = max(quarter // 2, 1)
            far = flip(gx, 2 * quarter + n, gx_bits)
            y, k = lax.div(lax.rem(n, quarter), row), lax.rem(n, row)
            x = jnp.where(lax.rem(gx, quarter) < row, lax.rem(far, row), k)
            far = far - lax.rem(far, quarter) + y * row + x
            send_lags_to(far)

            @pl.when(n > 0)
            def _():
                send_lags_to(flip(gx, n, gx_bits))

            return carry

        lax.fori_loop(0, 2 * quarter, send_lags, 0)
        pltpu.make_async_copy(
            hbuf.at[ch, pl.ds(pl.multiple_of(gx * lag_rows, lag_rows), lag_rows)], hrecv.at[ch, gx], h_recv.at[ch, lax.div(gx, GROUP)]
        ).start()

    own_group = lax.div(gx, GROUP)
    zero = jnp.zeros((gx_size, HALF), bf16)
    left = lax.broadcasted_iota(jnp.int32, (gx_size, HALF), 1) == 0

    for ch in range(owned):

        def finish(n, carry):
            group = flip(own_group, n, (gx_size // GROUP).bit_length() - 1)
            sources = pl.ds(group * GROUP, GROUP)
            landed = hrecv.at[ch, sources]
            pltpu.make_async_copy(landed, landed, h_recv.at[ch, group]).wait()
            for part in range(2):
                x = hrecv[ch, sources, :, part * NB : (part + 1) * NB].reshape(GROUP * lag_rows, NB)
                y = dot(x, to[0]) + dot(x, to[1])
                out_ref[part, sources, ch] = y.reshape(GROUP, lag_rows, NB)
            return carry

        lax.fori_loop(0, gx_size // GROUP, finish, 0)

        @pl.when(gx == 0)
        def _():
            row = hrecv[ch, :, 0, :]
            a_hi, s1, a_lo, s3 = (row[:, k * HALF : (k + 1) * HALF] for k in range(4))
            for part in range(2):
                total = 0.0
                for a, b in ((a_hi, s1), (a_lo, s3)):
                    x = [a, jnp.where(left, b, zero)] if part == 0 else [zero, jnp.where(left, zero, b)]
                    x = jnp.concatenate(x, axis=1)
                    total += dot(x, to[0]) + dot(x, to[1])
                out_ref[part, :, ch, 0, :] = total

    for ch in range(owned):
        sent = hbuf.at[ch, pl.ds(0, (gx_size - 1) * lag_rows)]
        pltpu.make_async_copy(sent, sent, h_send.at[ch]).wait()
    sent = v_ref.at[:, pl.ds(0, channels - owned)]
    pltpu.make_async_copy(sent, sent, v_send).wait()


def fused(gx_size, gy_size, voltages):
    _, channels, snaps, _, _ = voltages.shape
    owned = channels // (gx_size * gy_size)
    lag_rows = NB // gx_size
    tables = [jnp.asarray(table) for table in fixed_tables()]
    bf16, f32 = jnp.bfloat16, jnp.float32
    dma = pltpu.SemaphoreType.DMA
    out = pl.pallas_call(
        functools.partial(kernel, gx_size, gy_size),
        out_shape=pltpu.VMEM((2, gx_size, owned, lag_rows, NB), f32),
        in_specs=[pl.BlockSpec(memory_space=pltpu.HBM)] * 6,
        out_specs=pl.BlockSpec(memory_space=pltpu.VMEM),
        scratch_shapes=[
            pltpu.VMEM((owned, 2, snaps, NA, NA), bf16),
            *[pltpu.VMEM(table.shape, bf16) for table in tables],
            pltpu.VMEM((HALF, NB), f32),
            pltpu.VMEM((HALF, NB), f32),
            pltpu.VMEM((8, NB), f32),
            pltpu.VMEM((owned, NB, 2 * NB), bf16),
            pltpu.VMEM((owned, gx_size, lag_rows, 2 * NB), bf16),
            pltpu.SemaphoreType.REGULAR,
            dma((5,)),
            dma,
            dma((owned * snaps // T_PART,)),
            dma((owned,)),
            dma((owned, gx_size // GROUP)),
        ],
        compiler_params=pltpu.CompilerParams(
            collective_id=0, has_side_effects=True, vmem_limit_bytes=40 * 2**20
        ),
        cost_estimate=pl.CostEstimate(flops=2 * 10**10, bytes_accessed=12 * 2**20, transcendentals=0),
    )(*[pltpu.with_memory_space_constraint(x, pltpu.HBM) for x in (voltages, *tables)])
    return out.reshape(2, gx_size * owned, lag_rows, NB)


def local(gx_size, gy_size, voltages):
    _, channels, snaps, x_rows, y_cols = voltages.shape
    count = gx_size * gy_size
    even_split = count & (count - 1) == 0 and gx_size >= 4 and gy_size == 2 and channels % count == 0
    whole_tiles = x_rows % 16 == 0 and y_cols % 128 == 0 and (NB // gx_size) % 16 == 0 and snaps % T_PART == 0
    if even_split and whole_tiles:
        return fused(gx_size, gy_size, voltages)
    return plain(voltages)


def solution(mesh):
    return jax.shard_map(
        functools.partial(local, mesh.shape["gx"], mesh.shape["gy"]),
        mesh=mesh,
        in_specs=(P(None, "grp", None, "gx", "gy"),),
        out_specs=P(None, ("grp", "gy"), "gx", None),
        check_vma=False,
    )
```

```python
import functools
import math

import jax
import jax.numpy as jnp
import ml_dtypes
import numpy as np
from jax import lax
from jax.experimental import pallas as pl
from jax.experimental.pallas import tpu as pltpu
from jax.sharding import PartitionSpec as P

NA = 256
T_SIZE = 8
NB = 512


def dft_table(row_count, col_count, sign_factor, scale_factor, out_type):
    row_index = lax.iota(jnp.int32, row_count)[:, None]
    col_index = lax.iota(jnp.int32, col_count)[None, :]
    phase_index = row_index * col_index % NB
    angles = 2.0 * math.pi / NB * phase_index.astype(jnp.float32)
    return (
        (jnp.cos(angles) * scale_factor).astype(out_type),
        (sign_factor * jnp.sin(angles) * scale_factor).astype(out_type),
    )


def plain(voltages):
    high = lax.Precision.HIGHEST
    f32 = jnp.float32
    fwd_re, fwd_im = dft_table(NA, NB, -1.0, 1.0, jnp.bfloat16)
    inv_re, inv_im = dft_table(NB, NB, 1.0, 1.0 / NB, jnp.float32)
    out_re, out_im = dft_table(NB, NB, 1.0, 1.0 / (NB * T_SIZE * NA), jnp.float32)
    turned = lax.all_to_all(voltages, "gy", split_axis=1, concat_axis=4, tiled=True)
    stacks, channels, snapshots, x_rows, y_cols = turned.shape
    gx_size = lax.axis_size("gx")
    item_count = channels * snapshots // gx_size
    group_snaps = min(item_count, snapshots)
    group_count = item_count // group_snaps
    item_rows = turned.reshape(2, channels * snapshots, x_rows, y_cols)
    received = lax.all_to_all(item_rows, "gx", split_axis=1, concat_axis=2, tiled=True)
    received = received.reshape(2, group_count, group_snaps, NA, NA)
    beam_re = jnp.einsum(
        "gtxy,yv->gtxv", received[0], fwd_re, preferred_element_type=f32
    ) - jnp.einsum("gtxy,yv->gtxv", received[1], fwd_im, preferred_element_type=f32)
    beam_im = jnp.einsum(
        "gtxy,yv->gtxv", received[0], fwd_im, preferred_element_type=f32
    ) + jnp.einsum("gtxy,yv->gtxv", received[1], fwd_re, preferred_element_type=f32)
    beam_re = beam_re.astype(jnp.bfloat16)
    beam_im = beam_im.astype(jnp.bfloat16)
    full_re = jnp.einsum("gtxv,xu->gtuv", beam_re, fwd_re, preferred_element_type=f32) - jnp.einsum(
        "gtxv,xu->gtuv", beam_im, fwd_im, preferred_element_type=f32
    )
    full_im = jnp.einsum("gtxv,xu->gtuv", beam_re, fwd_im, preferred_element_type=f32) + jnp.einsum(
        "gtxv,xu->gtuv", beam_im, fwd_re, preferred_element_type=f32
    )
    power = jnp.sum(full_re * full_re + full_im * full_im, axis=1)
    per_channel = gx_size * group_count // channels
    lag_re = jnp.einsum("guv,ul->glv", power, inv_re, precision=high)
    lag_im = jnp.einsum("guv,ul->glv", power, inv_im, precision=high)
    partial_value = jnp.stack([lag_re, lag_im], axis=1)[None]
    gathered_lags = lax.all_to_all(partial_value, "gx", split_axis=3, concat_axis=0, tiled=True)
    lag_rows_dev = gathered_lags.shape[3]
    lag_sums = jnp.sum(gathered_lags.reshape(channels, per_channel, 2, lag_rows_dev, NB), axis=1)
    vis_re = jnp.einsum("clv,vm->clm", lag_sums[:, 0], out_re, precision=high) - jnp.einsum(
        "clv,vm->clm", lag_sums[:, 1], out_im, precision=high
    )
    vis_im = jnp.einsum("clv,vm->clm", lag_sums[:, 0], out_im, precision=high) + jnp.einsum(
        "clv,vm->clm", lag_sums[:, 1], out_re, precision=high
    )
    return jnp.stack([vis_re, vis_im])


HALF = NB // 2
MESH = pl.DeviceIdType.MESH
T_PART = 4
GROUP = 4


def pair_of(x):
    high = x.astype(ml_dtypes.bfloat16)
    return np.stack([high, (x - high.astype(np.float64)).astype(ml_dtypes.bfloat16)])


def fixed_tables():
    turn = 2.0 * np.pi / NB
    a, b = np.arange(NA), np.arange(HALF)
    cos = np.cos(turn * (np.outer(a, b) % NB))
    sin = np.sin(turn * (np.outer(a, b) % NB))
    alt = 1.0 - 2.0 * (np.arange(NB) % 2)
    sin[:, 0] = alt[:NA]
    first = np.concatenate([cos, sin], axis=1).astype(ml_dtypes.bfloat16)
    second = np.ascontiguousarray(first.T)
    lag = np.outer(np.arange(NB), b) % NB
    lag_cos = 2.0 * np.cos(turn * lag) / NB
    lag_cos[:, 0] = 1.0 / NB
    lag_sin = 4.0 * np.sin(turn * lag) / NB
    out_phase = lag.T
    out_sin = np.sin(turn * out_phase)
    out_sin[0] = alt
    out = np.concatenate([np.cos(turn * out_phase), out_sin]) / (NB * T_SIZE * NA)
    return first, second, pair_of(lag_cos), pair_of(lag_sin), pair_of(out)


def flip(value, mask, bits):
    out = 0
    for k in range(bits):
        unit = 2**k
        out = out + lax.rem(lax.div(value, unit) + lax.div(mask, unit), 2) * unit
    return out


def rest(x):
    return x - x.astype(jnp.bfloat16).astype(jnp.float32)


def kernel(gx_size, gy_size, v_ref, t1_ref, t2_ref, tc_ref, ts_ref, to_ref, out_ref, rv, t1, t2, tc, ts, to, even, odd, nyq,
           hbuf, hrecv, all_in, tab_sem, v_send, v_recv, h_send, h_recv):
    f32, bf16 = jnp.float32, jnp.bfloat16
    _, channels, snaps, x_rows, y_cols = v_ref.shape
    count = gx_size * gy_size
    bits = count.bit_length() - 1
    owned = channels // count
    lag_rows = NB // gx_size
    grp, gx, gy = lax.axis_index("grp"), lax.axis_index("gx"), lax.axis_index("gy")
    me = gx * gy_size + gy
    parts = snaps // T_PART

    barrier = pltpu.get_barrier_semaphore()
    quarter = gx_size // 4
    gx_bits = gx_size.bit_length() - 1
    mirror = flip(gx, 3 * quarter, gx_bits)
    inner = lax.div(lax.rem(gx + quarter, gx_size), 2 * quarter) == 1

    @pl.when(inner)
    def _():
        for oy in range(gy_size):

            @pl.when(oy <= gy)
            def _():
                pl.semaphore_signal(barrier, inc=1, device_id=(grp, mirror, oy), device_id_type=MESH)


    for k in range(2 * quarter):
        outer = (3 * quarter + k) % gx_size
        for oy in range(gy_size):

            @pl.when((outer != gx) | (oy != gy))
            def _():
                pl.semaphore_signal(barrier, inc=1, device_id=(grp, outer, oy), device_id_type=MESH)

    x_at = pl.ds(pl.multiple_of(gx * x_rows, x_rows), x_rows)
    y_at = pl.ds(pl.multiple_of(gy * y_cols, y_cols), y_cols)

    def channel_of(ox, oy, ch):
        return oy * (channels // gy_size) + ox * owned + ch

    def send_block(ox, oy, ch, part):
        times = pl.ds(part * T_PART, T_PART)
        pltpu.make_async_remote_copy(
            src_ref=v_ref.at[:, channel_of(ox, oy, ch), times],
            dst_ref=rv.at[ch, :, times, x_at, y_at],
            send_sem=v_send,
            recv_sem=v_recv.at[ch * parts + part],
            device_id=(grp, ox, oy),
            device_id_type=MESH,
        ).start()

    @pl.when(inner)
    def _():
        pl.semaphore_wait(barrier, gy_size - gy)
        for ch in range(owned):
            for part in range(parts):
                for oy in range(gy_size):

                    @pl.when(oy >= gy)
                    def _():
                        send_block(mirror, oy, ch, part)


    tables = [
        pltpu.make_async_copy(src, dst, tab_sem.at[n])
        for n, (src, dst) in enumerate(((t1_ref, t1), (t2_ref, t2), (tc_ref, tc), (ts_ref, ts), (to_ref, to)))
    ]
    for copy in tables:
        copy.start()

    @pl.when(inner)
    def _():
        pl.semaphore_wait(all_in, 1)

    @pl.when(~inner)
    def _():
        pl.semaphore_wait(barrier, count - 1)
        pl.semaphore_signal(all_in, inc=1, device_id=(grp, flip(gx, quarter, gx_bits), gy), device_id_type=MESH)

    for ch in range(owned):
        for part in range(parts):
            times = pl.ds(part * T_PART, T_PART)

            def send(n, carry):
                s = lax.rem(n, 2) * (count // 2) + lax.div(n, 2)
                other = flip(me, s, bits)
                half_col = quarter * gy_size // 2
                m = lax.rem(lax.div(n, 2), quarter * gy_size)
                fixed = other - lax.rem(other, quarter * gy_size) + lax.div(m, half_col) * half_col + lax.rem(other, half_col)
                other = jnp.where(lax.rem(n, 2) == 1, fixed, other)

                @pl.when(~inner | (lax.div(other, gy_size) != mirror) | (lax.rem(other, gy_size) < gy))
                def _():
                    send_block(lax.div(other, gy_size), lax.rem(other, gy_size), ch, part)

                return carry

            lax.fori_loop(1, count, send, 0)
            pltpu.make_async_copy(
                v_ref.at[:, channel_of(gx, gy, ch), times], rv.at[ch, :, times, x_at, y_at], v_recv.at[ch * parts + part]
            ).start()

    for copy in tables:
        copy.wait()

    lane0 = lax.broadcasted_iota(jnp.int32, (NA, HALF), 1) == 0
    row0 = lax.broadcasted_iota(jnp.int32, (HALF, HALF), 0) == 0
    dot = functools.partial(jnp.dot, preferred_element_type=f32)

    for ch in range(owned):
        even[...] = jnp.zeros_like(even)
        odd[...] = jnp.zeros_like(odd)
        nyq[...] = jnp.zeros_like(nyq)
        for part in range(parts):
            landed = rv.at[ch, :, pl.ds(part * T_PART, T_PART)]
            pltpu.make_async_copy(landed, landed, v_recv.at[ch * parts + part]).wait()

            def snapshot(t, carry):
                re = dot(rv[ch, 0, t], t1[...])
                im = dot(rv[ch, 1, t], t1[...])
                cr, sr, ci, si = re[:, :HALF], re[:, HALF:], im[:, :HALF], im[:, HALF:]
                halves = (
                    (cr + jnp.where(lane0, 0.0, si), ci - jnp.where(lane0, 0.0, sr)),
                    (jnp.where(lane0, sr, cr - si), jnp.where(lane0, si, ci + sr)),
                )
                for n, (b_re, b_im) in enumerate(halves):
                    at = slice(n * HALF, (n + 1) * HALF)
                    re = dot(t2[...], b_re.astype(bf16))
                    im = dot(t2[...], b_im.astype(bf16))
                    cr, sr, ci, si = re[:HALF], re[HALF:], im[:HALF], im[HALF:]
                    nyq[:, at] += sr[:8] * sr[:8] + si[:8] * si[:8]
                    sr, si = jnp.where(row0, 0.0, sr), jnp.where(row0, 0.0, si)
                    even[:, at] += (cr * cr + ci * ci) + (sr * sr + si * si)
                    odd[:, at] += cr * si - ci * sr
                return carry

            lax.fori_loop(part * T_PART, (part + 1) * T_PART, snapshot, 0)

        e_hi = even[...].astype(bf16)
        e_lo = (even[...] - e_hi.astype(f32)).astype(bf16)
        o_hi = odd[...].astype(bf16)
        o_lo = (odd[...] - o_hi.astype(f32)).astype(bf16)
        alt = 1.0 - 2.0 * lax.rem(lax.broadcasted_iota(jnp.int32, (HALF, 1), 0), 2).astype(f32)
        top = nyq[0:1, :] * (1.0 / NB)
        mask = lax.broadcasted_iota(jnp.int32, (HALF, HALF), 1) == 0
        for n in range(2):
            rows = slice(n * HALF, (n + 1) * HALF)
            h_re = dot(tc[0, rows], e_hi) + dot(tc[0, rows], e_lo) + dot(tc[1, rows], e_hi) + alt * top
            h_im = dot(ts[0, rows], o_hi) + dot(ts[0, rows], o_lo) + dot(ts[1, rows], o_hi)
            rp, rm, ip, im = h_re[:, :HALF], h_re[:, HALF:], h_im[:, :HALF], h_im[:, HALF:]
            slots = [
                jnp.where(mask, rp, rp + rm),
                jnp.where(mask, rm, im - ip),
                jnp.where(mask, ip, ip + im),
                jnp.where(mask, im, rp - rm),
            ]
            if n == 0:
                slots[1] = jnp.where(row0 & ~mask, rest(rp - rm), slots[1])
                slots[2] = jnp.where(row0, rest(slots[0]), slots[2])
                slots[3] = jnp.where(row0 & mask, rest(rm), slots[3])
            for k, slot in enumerate(slots):
                hbuf[ch, rows, k * HALF : (k + 1) * HALF] = slot.astype(bf16)

        def send_lags_to(other):
            pltpu.make_async_remote_copy(
                src_ref=hbuf.at[ch, pl.ds(pl.multiple_of(other * lag_rows, lag_rows), lag_rows)],
                dst_ref=hrecv.at[ch, gx],
                send_sem=h_send.at[ch],
                recv_sem=h_recv.at[ch, lax.div(gx, GROUP)],
                device_id=(grp, other, gy),
                device_id_type=MESH,
            ).start()

        def send_lags(n, carry):
            row = max(quarter // 2, 1)
            far = flip(gx, 2 * quarter + n, gx_bits)
            y, k = lax.div(lax.rem(n, quarter), row), lax.rem(n, row)
            x = jnp.where((y == 0) | (lax.rem(gx, quarter) < row), lax.rem(far, row), k)
            far = far - lax.rem(far, quarter) + y * row + x
            send_lags_to(far)

            @pl.when(n > 0)
            def _():
                send_lags_to(flip(gx, n, gx_bits))

            return carry

        lax.fori_loop(0, 2 * quarter, send_lags, 0)
        pltpu.make_async_copy(
            hbuf.at[ch, pl.ds(pl.multiple_of(gx * lag_rows, lag_rows), lag_rows)], hrecv.at[ch, gx], h_recv.at[ch, lax.div(gx, GROUP)]
        ).start()

    own_group = lax.div(gx, GROUP)
    zero = jnp.zeros((gx_size, HALF), bf16)
    left = lax.broadcasted_iota(jnp.int32, (gx_size, HALF), 1) == 0

    for ch in range(owned):

        def finish(n, carry):
            group = flip(own_group, n, (gx_size // GROUP).bit_length() - 1)
            sources = pl.ds(group * GROUP, GROUP)
            landed = hrecv.at[ch, sources]
            pltpu.make_async_copy(landed, landed, h_recv.at[ch, group]).wait()
            for part in range(2):
                x = hrecv[ch, sources, :, part * NB : (part + 1) * NB].reshape(GROUP * lag_rows, NB)
                y = dot(x, to[0]) + dot(x, to[1])
                out_ref[part, sources, ch] = y.reshape(GROUP, lag_rows, NB)
            return carry

        lax.fori_loop(0, gx_size // GROUP, finish, 0)

        @pl.when(gx == 0)
        def _():
            row = hrecv[ch, :, 0, :]
            a_hi, s1, a_lo, s3 = (row[:, k * HALF : (k + 1) * HALF] for k in range(4))
            for part in range(2):
                total = 0.0
                for a, b in ((a_hi, s1), (a_lo, s3)):
                    x = [a, jnp.where(left, b, zero)] if part == 0 else [zero, jnp.where(left, zero, b)]
                    x = jnp.concatenate(x, axis=1)
                    total += dot(x, to[0]) + dot(x, to[1])
                out_ref[part, :, ch, 0, :] = total

    for ch in range(owned):
        sent = hbuf.at[ch, pl.ds(0, (gx_size - 1) * lag_rows)]
        pltpu.make_async_copy(sent, sent, h_send.at[ch]).wait()
    sent = v_ref.at[:, pl.ds(0, channels - owned)]
    pltpu.make_async_copy(sent, sent, v_send).wait()


def fused(gx_size, gy_size, voltages):
    _, channels, snaps, _, _ = voltages.shape
    owned = channels // (gx_size * gy_size)
    lag_rows = NB // gx_size
    tables = [jnp.asarray(table) for table in fixed_tables()]
    bf16, f32 = jnp.bfloat16, jnp.float32
    dma = pltpu.SemaphoreType.DMA
    out = pl.pallas_call(
        functools.partial(kernel, gx_size, gy_size),
        out_shape=pltpu.VMEM((2, gx_size, owned, lag_rows, NB), f32),
        in_specs=[pl.BlockSpec(memory_space=pltpu.HBM)] * 6,
        out_specs=pl.BlockSpec(memory_space=pltpu.VMEM),
        scratch_shapes=[
            pltpu.VMEM((owned, 2, snaps, NA, NA), bf16),
            *[pltpu.VMEM(table.shape, bf16) for table in tables],
            pltpu.VMEM((HALF, NB), f32),
            pltpu.VMEM((HALF, NB), f32),
            pltpu.VMEM((8, NB), f32),
            pltpu.VMEM((owned, NB, 2 * NB), bf16),
            pltpu.VMEM((owned, gx_size, lag_rows, 2 * NB), bf16),
            pltpu.SemaphoreType.REGULAR,
            dma((5,)),
            dma,
            dma((owned * snaps // T_PART,)),
            dma((owned,)),
            dma((owned, gx_size // GROUP)),
        ],
        compiler_params=pltpu.CompilerParams(
            collective_id=0, has_side_effects=True, vmem_limit_bytes=40 * 2**20
        ),
        cost_estimate=pl.CostEstimate(flops=2 * 10**10, bytes_accessed=12 * 2**20, transcendentals=0),
    )(*[pltpu.with_memory_space_constraint(x, pltpu.HBM) for x in (voltages, *tables)])
    return out.reshape(2, gx_size * owned, lag_rows, NB)


def local(gx_size, gy_size, voltages):
    _, channels, snaps, x_rows, y_cols = voltages.shape
    count = gx_size * gy_size
    even_split = count & (count - 1) == 0 and gx_size >= 4 and gy_size == 2 and channels % count == 0
    whole_tiles = x_rows % 16 == 0 and y_cols % 128 == 0 and (NB // gx_size) % 16 == 0 and snaps % T_PART == 0
    if even_split and whole_tiles:
        return fused(gx_size, gy_size, voltages)
    return plain(voltages)


def solution(mesh):
    return jax.shard_map(
        functools.partial(local, mesh.shape["gx"], mesh.shape["gy"]),
        mesh=mesh,
        in_specs=(P(None, "grp", None, "gx", "gy"),),
        out_specs=P(None, ("grp", "gy"), "gx", None),
        check_vma=False,
    )
```

```python
import functools
import math

import jax
import jax.numpy as jnp
import ml_dtypes
import numpy as np
from jax import lax
from jax.experimental import pallas as pl
from jax.experimental.pallas import tpu as pltpu
from jax.sharding import PartitionSpec as P

NA = 256
T_SIZE = 8
NB = 512


def dft_table(row_count, col_count, sign_factor, scale_factor, out_type):
    row_index = lax.iota(jnp.int32, row_count)[:, None]
    col_index = lax.iota(jnp.int32, col_count)[None, :]
    phase_index = row_index * col_index % NB
    angles = 2.0 * math.pi / NB * phase_index.astype(jnp.float32)
    return (
        (jnp.cos(angles) * scale_factor).astype(out_type),
        (sign_factor * jnp.sin(angles) * scale_factor).astype(out_type),
    )


def plain(voltages):
    high = lax.Precision.HIGHEST
    f32 = jnp.float32
    fwd_re, fwd_im = dft_table(NA, NB, -1.0, 1.0, jnp.bfloat16)
    inv_re, inv_im = dft_table(NB, NB, 1.0, 1.0 / NB, jnp.float32)
    out_re, out_im = dft_table(NB, NB, 1.0, 1.0 / (NB * T_SIZE * NA), jnp.float32)
    turned = lax.all_to_all(voltages, "gy", split_axis=1, concat_axis=4, tiled=True)
    stacks, channels, snapshots, x_rows, y_cols = turned.shape
    gx_size = lax.axis_size("gx")
    item_count = channels * snapshots // gx_size
    group_snaps = min(item_count, snapshots)
    group_count = item_count // group_snaps
    item_rows = turned.reshape(2, channels * snapshots, x_rows, y_cols)
    received = lax.all_to_all(item_rows, "gx", split_axis=1, concat_axis=2, tiled=True)
    received = received.reshape(2, group_count, group_snaps, NA, NA)
    beam_re = jnp.einsum(
        "gtxy,yv->gtxv", received[0], fwd_re, preferred_element_type=f32
    ) - jnp.einsum("gtxy,yv->gtxv", received[1], fwd_im, preferred_element_type=f32)
    beam_im = jnp.einsum(
        "gtxy,yv->gtxv", received[0], fwd_im, preferred_element_type=f32
    ) + jnp.einsum("gtxy,yv->gtxv", received[1], fwd_re, preferred_element_type=f32)
    beam_re = beam_re.astype(jnp.bfloat16)
    beam_im = beam_im.astype(jnp.bfloat16)
    full_re = jnp.einsum("gtxv,xu->gtuv", beam_re, fwd_re, preferred_element_type=f32) - jnp.einsum(
        "gtxv,xu->gtuv", beam_im, fwd_im, preferred_element_type=f32
    )
    full_im = jnp.einsum("gtxv,xu->gtuv", beam_re, fwd_im, preferred_element_type=f32) + jnp.einsum(
        "gtxv,xu->gtuv", beam_im, fwd_re, preferred_element_type=f32
    )
    power = jnp.sum(full_re * full_re + full_im * full_im, axis=1)
    per_channel = gx_size * group_count // channels
    lag_re = jnp.einsum("guv,ul->glv", power, inv_re, precision=high)
    lag_im = jnp.einsum("guv,ul->glv", power, inv_im, precision=high)
    partial_value = jnp.stack([lag_re, lag_im], axis=1)[None]
    gathered_lags = lax.all_to_all(partial_value, "gx", split_axis=3, concat_axis=0, tiled=True)
    lag_rows_dev = gathered_lags.shape[3]
    lag_sums = jnp.sum(gathered_lags.reshape(channels, per_channel, 2, lag_rows_dev, NB), axis=1)
    vis_re = jnp.einsum("clv,vm->clm", lag_sums[:, 0], out_re, precision=high) - jnp.einsum(
        "clv,vm->clm", lag_sums[:, 1], out_im, precision=high
    )
    vis_im = jnp.einsum("clv,vm->clm", lag_sums[:, 0], out_im, precision=high) + jnp.einsum(
        "clv,vm->clm", lag_sums[:, 1], out_re, precision=high
    )
    return jnp.stack([vis_re, vis_im])


HALF = NB // 2
MESH = pl.DeviceIdType.MESH
T_PART = 4
GROUP = 4


def pair_of(x):
    high = x.astype(ml_dtypes.bfloat16)
    return np.stack([high, (x - high.astype(np.float64)).astype(ml_dtypes.bfloat16)])


def fixed_tables():
    turn = 2.0 * np.pi / NB
    a, b = np.arange(NA), np.arange(HALF)
    cos = np.cos(turn * (np.outer(a, b) % NB))
    sin = np.sin(turn * (np.outer(a, b) % NB))
    alt = 1.0 - 2.0 * (np.arange(NB) % 2)
    sin[:, 0] = alt[:NA]
    first = np.concatenate([cos, sin], axis=1).astype(ml_dtypes.bfloat16)
    second = np.ascontiguousarray(first.T)
    lag = np.outer(np.arange(NB), b) % NB
    lag_cos = 2.0 * np.cos(turn * lag) / NB
    lag_cos[:, 0] = 1.0 / NB
    lag_sin = 4.0 * np.sin(turn * lag) / NB
    out_phase = lag.T
    out_sin = np.sin(turn * out_phase)
    out_sin[0] = alt
    out = np.concatenate([np.cos(turn * out_phase), out_sin]) / (NB * T_SIZE * NA)
    return first, second, pair_of(lag_cos), pair_of(lag_sin), pair_of(out)


def flip(value, mask, bits):
    out = 0
    for k in range(bits):
        unit = 2**k
        out = out + lax.rem(lax.div(value, unit) + lax.div(mask, unit), 2) * unit
    return out


def rest(x):
    return x - x.astype(jnp.bfloat16).astype(jnp.float32)


def kernel(gx_size, gy_size, v_ref, t1_ref, t2_ref, tc_ref, ts_ref, to_ref, out_ref, rv, t1, t2, tc, ts, to, even, odd, nyq,
           hbuf, hrecv, all_in, tab_sem, v_send, v_recv, h_send, h_recv):
    f32, bf16 = jnp.float32, jnp.bfloat16
    _, channels, snaps, x_rows, y_cols = v_ref.shape
    count = gx_size * gy_size
    bits = count.bit_length() - 1
    owned = channels // count
    lag_rows = NB // gx_size
    grp, gx, gy = lax.axis_index("grp"), lax.axis_index("gx"), lax.axis_index("gy")
    me = gx * gy_size + gy
    parts = snaps // T_PART

    barrier = pltpu.get_barrier_semaphore()
    quarter = gx_size // 4
    gx_bits = gx_size.bit_length() - 1
    mirror = flip(gx, 3 * quarter, gx_bits)
    inner = lax.div(lax.rem(gx + quarter, gx_size), 2 * quarter) == 1

    @pl.when(inner)
    def _():
        for oy in range(gy_size):

            @pl.when(oy <= gy)
            def _():
                pl.semaphore_signal(barrier, inc=1, device_id=(grp, mirror, oy), device_id_type=MESH)


    for k in range(2 * quarter):
        outer = (3 * quarter + k) % gx_size
        for oy in range(gy_size):

            @pl.when((outer != gx) | (oy != gy))
            def _():
                pl.semaphore_signal(barrier, inc=1, device_id=(grp, outer, oy), device_id_type=MESH)

    x_at = pl.ds(pl.multiple_of(gx * x_rows, x_rows), x_rows)
    y_at = pl.ds(pl.multiple_of(gy * y_cols, y_cols), y_cols)

    def channel_of(ox, oy, ch):
        return oy * (channels // gy_size) + ox * owned + ch

    def send_block(ox, oy, ch, part):
        times = pl.ds(part * T_PART, T_PART)
        pltpu.make_async_remote_copy(
            src_ref=v_ref.at[:, channel_of(ox, oy, ch), times],
            dst_ref=rv.at[ch, :, times, x_at, y_at],
            send_sem=v_send,
            recv_sem=v_recv.at[ch * parts + part],
            device_id=(grp, ox, oy),
            device_id_type=MESH,
        ).start()

    @pl.when(inner)
    def _():
        pl.semaphore_wait(barrier, gy_size - gy)
        for ch in range(owned):
            for part in range(parts):
                for oy in range(gy_size):

                    @pl.when(oy >= gy)
                    def _():
                        send_block(mirror, oy, ch, part)


    tables = [
        pltpu.make_async_copy(src, dst, tab_sem.at[n])
        for n, (src, dst) in enumerate(((t1_ref, t1), (t2_ref, t2), (tc_ref, tc), (ts_ref, ts), (to_ref, to)))
    ]
    for copy in tables:
        copy.start()

    @pl.when(inner)
    def _():
        pl.semaphore_wait(all_in, 1)

    @pl.when(~inner)
    def _():
        pl.semaphore_wait(barrier, count - 1)
        pl.semaphore_signal(all_in, inc=1, device_id=(grp, flip(gx, quarter, gx_bits), gy), device_id_type=MESH)

    for ch in range(owned):
        for part in range(parts):
            times = pl.ds(part * T_PART, T_PART)

            def send(n, carry):
                k = lax.div(n, 2)
                block = quarter * gy_size
                k = jnp.where(lax.rem(n, 2) == 1, lax.rem(k, 2) * block + lax.div(k, 2), k)
                s = lax.rem(n, 2) * (count // 2) + k
                other = flip(me, s, bits)

                @pl.when(~inner | (lax.div(s, gy_size) != 3 * quarter) | (lax.rem(other, gy_size) < gy))
                def _():
                    send_block(lax.div(other, gy_size), lax.rem(other, gy_size), ch, part)

                return carry

            lax.fori_loop(1, count, send, 0)
            pltpu.make_async_copy(
                v_ref.at[:, channel_of(gx, gy, ch), times], rv.at[ch, :, times, x_at, y_at], v_recv.at[ch * parts + part]
            ).start()

    for copy in tables:
        copy.wait()

    lane0 = lax.broadcasted_iota(jnp.int32, (NA, HALF), 1) == 0
    row0 = lax.broadcasted_iota(jnp.int32, (HALF, HALF), 0) == 0
    dot = functools.partial(jnp.dot, preferred_element_type=f32)

    for ch in range(owned):
        even[...] = jnp.zeros_like(even)
        odd[...] = jnp.zeros_like(odd)
        nyq[...] = jnp.zeros_like(nyq)
        for part in range(parts):
            landed = rv.at[ch, :, pl.ds(part * T_PART, T_PART)]
            pltpu.make_async_copy(landed, landed, v_recv.at[ch * parts + part]).wait()

            def snapshot(t, carry):
                re = dot(rv[ch, 0, t], t1[...])
                im = dot(rv[ch, 1, t], t1[...])
                cr, sr, ci, si = re[:, :HALF], re[:, HALF:], im[:, :HALF], im[:, HALF:]
                halves = (
                    (cr + jnp.where(lane0, 0.0, si), ci - jnp.where(lane0, 0.0, sr)),
                    (jnp.where(lane0, sr, cr - si), jnp.where(lane0, si, ci + sr)),
                )
                for n, (b_re, b_im) in enumerate(halves):
                    at = slice(n * HALF, (n + 1) * HALF)
                    re = dot(t2[...], b_re.astype(bf16))
                    im = dot(t2[...], b_im.astype(bf16))
                    cr, sr, ci, si = re[:HALF], re[HALF:], im[:HALF], im[HALF:]
                    nyq[:, at] += sr[:8] * sr[:8] + si[:8] * si[:8]
                    sr, si = jnp.where(row0, 0.0, sr), jnp.where(row0, 0.0, si)
                    even[:, at] += (cr * cr + ci * ci) + (sr * sr + si * si)
                    odd[:, at] += cr * si - ci * sr
                return carry

            lax.fori_loop(part * T_PART, (part + 1) * T_PART, snapshot, 0)

        e_hi = even[...].astype(bf16)
        e_lo = (even[...] - e_hi.astype(f32)).astype(bf16)
        o_hi = odd[...].astype(bf16)
        o_lo = (odd[...] - o_hi.astype(f32)).astype(bf16)
        alt = 1.0 - 2.0 * lax.rem(lax.broadcasted_iota(jnp.int32, (HALF, 1), 0), 2).astype(f32)
        top = nyq[0:1, :] * (1.0 / NB)
        mask = lax.broadcasted_iota(jnp.int32, (HALF, HALF), 1) == 0
        for n in range(2):
            rows = slice(n * HALF, (n + 1) * HALF)
            h_re = dot(tc[0, rows], e_hi) + dot(tc[0, rows], e_lo) + dot(tc[1, rows], e_hi) + alt * top
            h_im = dot(ts[0, rows], o_hi) + dot(ts[0, rows], o_lo) + dot(ts[1, rows], o_hi)
            rp, rm, ip, im = h_re[:, :HALF], h_re[:, HALF:], h_im[:, :HALF], h_im[:, HALF:]
            slots = [
                jnp.where(mask, rp, rp + rm),
                jnp.where(mask, rm, im - ip),
                jnp.where(mask, ip, ip + im),
                jnp.where(mask, im, rp - rm),
            ]
            if n == 0:
                slots[1] = jnp.where(row0 & ~mask, rest(rp - rm), slots[1])
                slots[2] = jnp.where(row0, rest(slots[0]), slots[2])
                slots[3] = jnp.where(row0 & mask, rest(rm), slots[3])
            for k, slot in enumerate(slots):
                hbuf[ch, rows, k * HALF : (k + 1) * HALF] = slot.astype(bf16)

        def send_lags_to(other):
            pltpu.make_async_remote_copy(
                src_ref=hbuf.at[ch, pl.ds(pl.multiple_of(other * lag_rows, lag_rows), lag_rows)],
                dst_ref=hrecv.at[ch, gx],
                send_sem=h_send.at[ch],
                recv_sem=h_recv.at[ch, lax.div(gx, GROUP)],
                device_id=(grp, other, gy),
                device_id_type=MESH,
            ).start()

        def send_lags(n, carry):
            row = max(quarter // 2, 1)
            far = flip(gx, 2 * quarter + n, gx_bits)
            y, k = lax.div(lax.rem(n, quarter), row), lax.rem(n, row)
            x = jnp.where((y == 0) | (lax.rem(gx, quarter) < row), lax.rem(far, row), k)
            far = far - lax.rem(far, quarter) + y * row + x
            send_lags_to(far)

            @pl.when(n > 0)
            def _():
                send_lags_to(flip(gx, n, gx_bits))

            return carry

        lax.fori_loop(0, 2 * quarter, send_lags, 0)
        pltpu.make_async_copy(
            hbuf.at[ch, pl.ds(pl.multiple_of(gx * lag_rows, lag_rows), lag_rows)], hrecv.at[ch, gx], h_recv.at[ch, lax.div(gx, GROUP)]
        ).start()

    own_group = lax.div(gx, GROUP)
    zero = jnp.zeros((gx_size, HALF), bf16)
    left = lax.broadcasted_iota(jnp.int32, (gx_size, HALF), 1) == 0

    for ch in range(owned):

        def finish(n, carry):
            group = flip(own_group, n, (gx_size // GROUP).bit_length() - 1)
            sources = pl.ds(group * GROUP, GROUP)
            landed = hrecv.at[ch, sources]
            pltpu.make_async_copy(landed, landed, h_recv.at[ch, group]).wait()
            for part in range(2):
                x = hrecv[ch, sources, :, part * NB : (part + 1) * NB].reshape(GROUP * lag_rows, NB)
                y = dot(x, to[0]) + dot(x, to[1])
                out_ref[part, sources, ch] = y.reshape(GROUP, lag_rows, NB)
            return carry

        lax.fori_loop(0, gx_size // GROUP, finish, 0)

        @pl.when(gx == 0)
        def _():
            row = hrecv[ch, :, 0, :]
            a_hi, s1, a_lo, s3 = (row[:, k * HALF : (k + 1) * HALF] for k in range(4))
            for part in range(2):
                total = 0.0
                for a, b in ((a_hi, s1), (a_lo, s3)):
                    x = [a, jnp.where(left, b, zero)] if part == 0 else [zero, jnp.where(left, zero, b)]
                    x = jnp.concatenate(x, axis=1)
                    total += dot(x, to[0]) + dot(x, to[1])
                out_ref[part, :, ch, 0, :] = total

    for ch in range(owned):
        sent = hbuf.at[ch, pl.ds(0, (gx_size - 1) * lag_rows)]
        pltpu.make_async_copy(sent, sent, h_send.at[ch]).wait()
    sent = v_ref.at[:, pl.ds(0, channels - owned)]
    pltpu.make_async_copy(sent, sent, v_send).wait()


def fused(gx_size, gy_size, voltages):
    _, channels, snaps, _, _ = voltages.shape
    owned = channels // (gx_size * gy_size)
    lag_rows = NB // gx_size
    tables = [jnp.asarray(table) for table in fixed_tables()]
    bf16, f32 = jnp.bfloat16, jnp.float32
    dma = pltpu.SemaphoreType.DMA
    out = pl.pallas_call(
        functools.partial(kernel, gx_size, gy_size),
        out_shape=pltpu.VMEM((2, gx_size, owned, lag_rows, NB), f32),
        in_specs=[pl.BlockSpec(memory_space=pltpu.HBM)] * 6,
        out_specs=pl.BlockSpec(memory_space=pltpu.VMEM),
        scratch_shapes=[
            pltpu.VMEM((owned, 2, snaps, NA, NA), bf16),
            *[pltpu.VMEM(table.shape, bf16) for table in tables],
            pltpu.VMEM((HALF, NB), f32),
            pltpu.VMEM((HALF, NB), f32),
            pltpu.VMEM((8, NB), f32),
            pltpu.VMEM((owned, NB, 2 * NB), bf16),
            pltpu.VMEM((owned, gx_size, lag_rows, 2 * NB), bf16),
            pltpu.SemaphoreType.REGULAR,
            dma((5,)),
            dma,
            dma((owned * snaps // T_PART,)),
            dma((owned,)),
            dma((owned, gx_size // GROUP)),
        ],
        compiler_params=pltpu.CompilerParams(
            collective_id=0, has_side_effects=True, vmem_limit_bytes=40 * 2**20
        ),
        cost_estimate=pl.CostEstimate(flops=2 * 10**10, bytes_accessed=12 * 2**20, transcendentals=0),
    )(*[pltpu.with_memory_space_constraint(x, pltpu.HBM) for x in (voltages, *tables)])
    return out.reshape(2, gx_size * owned, lag_rows, NB)


def local(gx_size, gy_size, voltages):
    _, channels, snaps, x_rows, y_cols = voltages.shape
    count = gx_size * gy_size
    even_split = count & (count - 1) == 0 and gx_size >= 4 and gy_size == 2 and channels % count == 0
    whole_tiles = x_rows % 16 == 0 and y_cols % 128 == 0 and (NB // gx_size) % 16 == 0 and snaps % T_PART == 0
    if even_split and whole_tiles:
        return fused(gx_size, gy_size, voltages)
    return plain(voltages)


def solution(mesh):
    return jax.shard_map(
        functools.partial(local, mesh.shape["gx"], mesh.shape["gy"]),
        mesh=mesh,
        in_specs=(P(None, "grp", None, "gx", "gy"),),
        out_specs=P(None, ("grp", "gy"), "gx", None),
        check_vma=False,
    )
```
